128 devices in a mesh: tx: 16 (over x, z), ty: 8 (over y, core).
Axes of the slice: x: 4, y: 4, z: 4, core: 2. Of those that a mesh axis runs over, the one named last changes fastest.
Arguments:
- innovation: float32 [16384, 128], P(('tx', 'ty')), may hold values from -6 to 6
- obs_weight: float32 [16384, 128], P(('tx', 'ty')), may hold values from 0.5 to 4
- obs_operator: float32 [16384, 128, 128], P(('tx', 'ty')), may hold values from -0.5 to 0.5
- block_tile: int32 [16384, 1], P(('tx', 'ty')), may hold values from 0 to 15; in each aligned block of 128 rows (0 to 127, 128 to 255, ...) at most 24 rows name the same one
- owner_counts: int32 [128], P(('tx', 'ty')), may hold values from 64 to 128, as said below
- block_column: int32 [16384], P(('tx', 'ty')), may hold values from 0 to 255
- sea_mask: int32 [4, 1024, 1024], P(None, 'tx', 'ty'), may hold values 0 or 1
- diffusivity: float32 [4, 1024, 1024], P(None, 'tx', 'ty'), may hold values from 0.03 to 0.12
- background_std: float32 [4, 1024, 1024], P(None, 'tx', 'ty'), may hold values from 0.4 to 10.5
- step_counts: int32 [4], replicated, may hold values from 5 to 10, as said below
Outputs:
- control_field: float32 [4, 1024, 1024], P(None, 'tx', 'ty')
- residual: float32 [4, 1024, 1024], P(None, 'tx', 'ty')
The draws below stay inside these ranges and needn't reach their ends.
Inputs may be any that keep to these rules, and one draw needn't show every extreme that they name: `owner_counts`: at least one owner has all 128 blocks live. `step_counts`: at least one level takes 10 sweeps. `block_tile`: among the 128 blocks of one owner no tile index appears more than 24 times.
All inputs are finite; a program needn't handle non-finite values. No bound on the sum of `sea_mask` on one device may be relied on, other than what follows from the above.
Results may differ from the reference program's by a relative error of at most 0.04.
Values sent between devices are 32-bit elements; how exact they have to be, the bound alone decides.
No kernel may reach another device: no remote copies, remote signals or barrier semaphores. Data moves between devices by JAX's collectives and lax.ppermute only.
A program may use at most 192 MiB of HBM per device.

```python
import math
import jax
import jax.numpy as jnp
import numpy as np
from jax import lax

LEV = 4
CX = 64
CY = 128
OBLK = 128
NSTEP = 10
ITERS = 2
NX = 1024
NY = 1024
CAP = 24
BLOCKS = 16384
SEGS = 256
N_TX = 16
N_TY = 8


def draw_owner_counts(key, part):
    key = jax.random.fold_in(key, 11)
    first_key, second_key = jax.random.split(key)
    owners = N_TX * N_TY
    counts_drawn = jax.random.randint(first_key, (owners,), OBLK // 2, OBLK + 1, dtype=jnp.int32)
    full_owner = jax.random.randint(second_key, (), 0, owners, dtype=jnp.int32)
    return counts_drawn.at[full_owner].set(OBLK)


def draw_step_counts(key, part):
    key = jax.random.fold_in(key, 12)
    first_key, second_key = jax.random.split(key)
    counts_drawn = jax.random.randint(first_key, (LEV,), NSTEP // 2, NSTEP + 1, dtype=jnp.int32)
    full_level = jax.random.randint(second_key, (), 0, LEV, dtype=jnp.int32)
    return counts_drawn.at[full_level].set(NSTEP)


def draw_background_std(key, part):
    key = jax.random.fold_in(key, 13)
    roughness = jax.random.uniform(key, (LEV, NX, NY), jnp.float32, -0.8, 0.8)
    across = jnp.arange(NX, dtype=jnp.float32)[None, :, None] / max(NX - 1, 1)
    return jnp.exp(roughness + math.log(3.0) * across)


def place_ends(array, key, least, top_value):
    index_at = [jax.random.randint(jax.random.fold_in(key, axis), (), 0, length) for axis, length in enumerate(array.shape)]
    widest = array.shape.index(max(array.shape))
    next_to = index_at[:widest] + [(index_at[widest] + 1) % array.shape[widest]] + index_at[widest + 1:]
    return array.at[tuple(index_at)].set(least).at[tuple(next_to)].set(top_value)


def block_levels(own_key, extent, cuts, least, high):
    loudness = 1.0
    for dim, blocks in cuts:
        steps = jax.random.uniform(jax.random.fold_in(jax.random.fold_in(own_key, 6), dim), (blocks,), jnp.float32, least / len(cuts), high / len(cuts))
        loudness = loudness * jnp.repeat(jnp.exp(steps), extent[dim] // blocks).reshape((-1,) + (1,) * (len(extent) - 1 - dim))
    return loudness


def shared_out(stream_key, own, number, rows, number_of, top, most, skew):
    sequence = jax.random.permutation(stream_key, number_of)
    crowded, common = portions_of(number_of, rows * top, most, skew, True), portions_of(number_of, rows * top, most, skew, False)
    places = jnp.arange(number_of)

    def named(tallies, rotation):
        used = int((tallies > 0).sum())
        fixed = max(1, used // 4)
        passed = fixed + (places - fixed + rotation * (used - fixed)) % max(1, number_of - fixed)
        return jnp.zeros((number_of,), jnp.int32).at[sequence[jnp.where(places < fixed, places, passed)]].set(jnp.asarray(tallies, jnp.int32))

    tallies = jnp.where(number % 4 == 0, named(crowded, number // 4), named(common, number - number // 4 - 1))
    mixed = jax.random.permutation(jax.random.fold_in(own, 3), number_of)
    source_of, receiver = mixed[0:number_of // 2 * 2:2], mixed[1:number_of // 2 * 2:2]
    slack = jnp.minimum(tallies[source_of] - 1, most - tallies[receiver]) // 2
    slack = jnp.where((source_of == sequence[0]) | (receiver == sequence[0]) | (tallies[receiver] == 0), 0, jnp.maximum(slack, 0))
    passed = jax.random.randint(jax.random.fold_in(own, 4), (number_of // 2,), 0, 1 << 20) % (slack + 1)
    tallies = tallies.at[source_of].add(-passed).at[receiver].add(passed)
    members = jnp.searchsorted(jnp.cumsum(tallies), jnp.arange(rows * top), side="right").astype(jnp.int32)
    grid = members.reshape(top, rows).T
    grid = grid[jax.random.permutation(jax.random.fold_in(own, 1), rows)]
    rotation = jax.random.randint(jax.random.fold_in(own, 2), (rows, 1), 0, top)
    return jnp.take_along_axis(grid, (jnp.arange(top)[None, :] + rotation) % top, axis=1)


def portions_of(count, total, limit, lean, full):
    portions = [(1 << 20) // math.isqrt(standing ** lean) + 1 for standing in range(1, count + 1)]
    largest = limit if full else min(limit, max(-(-total // count), total * portions[0] // sum(portions)))
    least = 1 if total - largest >= count - 1 else 0
    counts, rest = [largest] + [least] * (count - 1), total - largest - least * (count - 1)
    while rest > 0:
        movable = [i for i in range(1, count) if counts[i] < largest] or [i for i in range(1, count) if counts[i] < limit]
        mass, left = sum([portions[i] for i in movable]), rest
        for i in movable:
            more = min(limit - counts[i], max(1, left * portions[i] // mass), rest)
            counts[i] = counts[i] + more
            rest = rest - more
    return np.array(counts)


def bell_draw(stream_key, dims, deviation, reach, pieces=(), held_as=jnp.bfloat16):
    entries = deviation * jax.random.normal(stream_key, dims, jnp.float32)
    if pieces:
        entries = entries * block_levels(stream_key, dims, pieces, -0.22, 0.18)
    return jnp.clip(entries, -reach, reach).astype(held_as)


def setup_inputs(seed: int = 0) -> dict:
    key_of = jax.random.split(jax.random.key(seed), 11)
    innovation = bell_draw(key_of[0], (BLOCKS, 128), 1.0, 6.0, ((0, 128),), jnp.float32)
    obs_weight = jnp.clip(jnp.exp(math.log(4.0) - 2.0794415 * jax.random.uniform(key_of[1], (BLOCKS, 128), jnp.float32) ** block_levels(key_of[1], (BLOCKS, 128), ((0, 128),), -0.2, 0.2)), 0.5, 4.0)
    obs_operator = bell_draw(key_of[2], (BLOCKS, 128, 128), 128 ** -0.5, 0.5, ((0, 128),), jnp.float32)
    block_tile_keys = jax.random.split(jax.random.fold_in(key_of[3], 1), BLOCKS // OBLK)
    block_tile_turns = jax.random.permutation(jax.random.fold_in(key_of[3], 3), BLOCKS // OBLK)
    block_tile = jax.vmap(lambda own, number: shared_out(jax.random.fold_in(key_of[3], 2), own, number, OBLK, N_TX, 1, CAP, 2))(block_tile_keys, block_tile_turns).reshape((BLOCKS, 1))
    owner_counts = draw_owner_counts(jax.random.fold_in(key_of[10], 71), 0)
    block_column = place_ends(jax.random.randint(key_of[5], (BLOCKS,), 0, SEGS), jax.random.fold_in(key_of[5], 1), 0, SEGS - 1).astype(jnp.int32)
    sea_mask = place_ends((jax.random.randint(key_of[6], (LEV, NX, NY), 0, 10) < 9).astype(jnp.int32), jax.random.fold_in(key_of[6], 1), 0, 1)
    diffusivity = jnp.clip(jnp.exp(math.log(0.12) - 1.3862944 * jax.random.uniform(key_of[7], (LEV, NX, NY), jnp.float32) ** block_levels(key_of[7], (LEV, NX, NY), ((1, 16), (2, 8)), -0.2, 0.2)), 0.03, 0.12)
    background_std = draw_background_std(jax.random.fold_in(key_of[10], 71), 0)
    step_counts = draw_step_counts(jax.random.fold_in(key_of[10], 71), 0)
    return {"innovation": innovation, "obs_weight": obs_weight, "obs_operator": obs_operator, "block_tile": block_tile, "owner_counts": owner_counts, "block_column": block_column, "sea_mask": sea_mask, "diffusivity": diffusivity, "background_std": background_std, "step_counts": step_counts}


def face_weights(mask_pad, kappa_pad):
    centre_m = mask_pad[:, 1:-1, 1:-1]
    centre_k = kappa_pad[:, 1:-1, 1:-1]
    east_face = 0.5 * (centre_m * kappa_pad[:, 2:, 1:-1] + centre_k * mask_pad[:, 2:, 1:-1])
    west_face = 0.5 * (mask_pad[:, :-2, 1:-1] * centre_k + kappa_pad[:, :-2, 1:-1] * centre_m)
    north_face = 0.5 * (centre_m * kappa_pad[:, 1:-1, 2:] + centre_k * mask_pad[:, 1:-1, 2:])
    south_face = 0.5 * (mask_pad[:, 1:-1, :-2] * centre_k + kappa_pad[:, 1:-1, :-2] * centre_m)
    return east_face, west_face, north_face, south_face


def diffusion_update(field_in, padded, face_set):
    east_face, west_face, north_face, south_face = face_set
    change = east_face * (padded[:, 2:, 1:-1] - field_in)
    change = change + west_face * (padded[:, :-2, 1:-1] - field_in)
    change = change + north_face * (padded[:, 1:-1, 2:] - field_in)
    change = change + south_face * (padded[:, 1:-1, :-2] - field_in)
    return field_in + change


def pad_sides(values):
    return jnp.pad(values, ((0, 0), (1, 1), (1, 1)))


def spread_field(field_in, mask_float, face_set, step_counts):
    current = field_in * mask_float
    for sweep_no in range(NSTEP):
        updated = diffusion_update(current, pad_sides(current), face_set)
        current = jnp.where((sweep_no < step_counts)[:, None, None], updated, current)
    return current


def to_segments(field_in):
    shaped = field_in.reshape(LEV, N_TX, CX, N_TY, CY // 128, 128)
    return shaped.transpose(1, 3, 0, 2, 4, 5).reshape(N_TX * N_TY * SEGS, 128)


def from_segments(segments):
    shaped = segments.reshape(N_TX, N_TY, LEV, CX, CY // 128, 128)
    return shaped.transpose(2, 0, 3, 1, 4, 5).reshape(LEV, NX, NY)


def reference(innovation, obs_weight, obs_operator, block_tile, owner_counts, block_column, sea_mask, diffusivity, background_std, step_counts):
    mask_float = sea_mask.astype(jnp.float32)
    kappa_masked = diffusivity * mask_float
    face_set = face_weights(pad_sides(mask_float), pad_sides(kappa_masked))
    row_index = jnp.arange(BLOCKS, dtype=jnp.int32)
    owner_index = row_index // OBLK
    band_index = owner_index % N_TY
    is_live = (row_index % OBLK) < owner_counts[owner_index]
    target = (block_tile[:, 0] * N_TY + band_index) * SEGS + block_column

    def spread_op(values):
        return spread_field(values, mask_float, face_set, step_counts)

    def adjoint(weighted):
        adjoint_cells = jnp.einsum('bij,bi->bj', obs_operator, weighted, precision=lax.Precision.HIGHEST)
        segments = jnp.zeros((N_TX * N_TY * SEGS, 128), jnp.float32).at[target].add(adjoint_cells)
        return from_segments(segments)

    def hessian(direction):
        spread = background_std * spread_op(direction)
        picked = to_segments(spread)[target]
        observed = jnp.einsum('bij,bj->bi', obs_operator, picked, precision=lax.Precision.HIGHEST)
        weighted = jnp.where(is_live[:, None], obs_weight * observed, 0.0)
        return direction + spread_op(background_std * adjoint(weighted))

    first_term = adjoint(jnp.where(is_live[:, None], obs_weight * innovation, 0.0))
    right_side = spread_op(background_std * first_term)
    control_field = jnp.zeros_like(right_side)
    residual = right_side
    direction = right_side
    norm_now = jnp.sum(residual * residual)
    for iter_no in range(ITERS):
        curved = hessian(direction)
        step_length = norm_now / jnp.sum(direction * curved)
        control_field = control_field + step_length * direction
        residual = residual - step_length * curved
        norm_next = jnp.sum(residual * residual)
        direction = residual + (norm_next / norm_now) * direction
        norm_now = norm_next
    return control_field, residual
```

```python
import jax
import jax.numpy as jnp
from jax import lax
from jax.experimental import pallas as pl
from jax.experimental.pallas import tpu as pltpu
from jax.sharding import PartitionSpec as P

F32 = jnp.float32
BF16 = jnp.bfloat16

LEV = 4
CX = 64
CY = 128
NSTEP = 10
MIN_STEPS = 5
HALO = 2 * NSTEP
SIDE = 24
EXT = CX + 2 * SIDE
ROWS = LEV * EXT
OWN = 128
TX = 16
TY = 8
CAP = 24
SLOTS = TX * CAP
LISTED = 3 * CAP
PART = 80
GROUP = 16
WIDE = 16
STRIP = 48
LAST = STRIP + 8


def iota(shape, dim):
    return lax.broadcasted_iota(jnp.int32, shape, dim)


def thirds(values):
    high = values.astype(BF16)
    rest = values - high.astype(F32)
    middle = rest.astype(BF16)
    low = (rest - middle.astype(F32)).astype(BF16)
    return high, middle, low


def pick(onehot, values):
    high, middle, low = thirds(values)
    total = jnp.dot(onehot, high, preferred_element_type=F32)
    total = total + jnp.dot(onehot, middle, preferred_element_type=F32)
    return total + jnp.dot(onehot, low, preferred_element_type=F32)


def as_onehot(hit):
    return jnp.where(hit, 1.0, 0.0).astype(BF16)


def slot_tables(tile_ref):
    down = iota((OWN, OWN), 0)
    across = iota((OWN, OWN), 1)
    tile_row = tile_ref[...].astype(F32)
    spread = jnp.broadcast_to(tile_row, (OWN, OWN))
    tile_col = jnp.sum(jnp.where(down == across, spread, 0.0), axis=1, keepdims=True)
    same = spread == tile_col
    rank_row = jnp.sum(jnp.where(same & (down < across), 1.0, 0.0), axis=0, keepdims=True)
    rank_col = jnp.sum(jnp.where(same & (across < down), 1.0, 0.0), axis=1, keepdims=True)
    return tile_row, rank_row, tile_col, rank_col


def write_parts(parts_ref, slots):
    for tile in range(TX):
        for side in (-1, 0, 1):
            source = tile + side
            rows = pl.ds((side + 1) * CAP, CAP)
            if 0 <= source < TX:
                parts_ref[tile, rows, :] = slots[source * CAP : (source + 1) * CAP]
            else:
                parts_ref[tile, rows, :] = jnp.zeros((CAP, 128), F32)


def to_slots(tables, adjoint):
    tile_row, rank_row, _, _ = tables
    slot_row = (tile_row * CAP + rank_row).astype(jnp.int32)
    return pick(as_onehot(iota((SLOTS, OWN), 0) == slot_row), adjoint)


def from_slots(tables, returned):
    _, _, tile_col, rank_col = tables
    slot_col = (tile_col * CAP + rank_col).astype(jnp.int32)
    return pick(as_onehot(iota((OWN, SLOTS), 1) == slot_col), returned)


def listed_columns(tables, column_ref):
    tile_row, _, _, rank_col = tables
    column_row = column_ref[...].astype(F32)
    tile_no = iota((TX, OWN), 0).astype(F32)
    lane = iota((OWN, 128), 1)
    rank = rank_col.astype(jnp.int32)
    total = jnp.zeros((TX, 128), F32)
    for side in (-1, 0, 1):
        mine = jnp.where(tile_row == tile_no + side, column_row, 0.0).astype(BF16)
        place = as_onehot(rank + (side + 1) * CAP == lane)
        total = total + jnp.dot(mine, place, preferred_element_type=F32)
    return total


def live_columns(count_ref, weighted):
    return jnp.where(iota((OWN, OWN), 1) < count_ref[0], weighted.T, 0.0)


def group_columns(columns_ref, step):
    turned = pltpu.roll(columns_ref[...], lax.rem(OWN - step * GROUP, OWN), 1)
    return turned[:, :GROUP]


def first_kernel(
    count_ref, tile_ref, column_ref, innovation_ref, weight_ref, operator_ref,
    parts_ref, adjoint_ref, columns_ref,
):
    step = pl.program_id(0)

    @pl.when(step == 0)
    def _():
        columns_ref[...] = live_columns(count_ref, weight_ref[...] * innovation_ref[...])

    columns = group_columns(columns_ref, step)
    rows = []
    for k in range(GROUP):
        rows.append(jnp.sum(operator_ref[k] * columns[:, k : k + 1], axis=0, keepdims=True))
    adjoint_ref[pl.ds(pl.multiple_of(step * GROUP, GROUP), GROUP), :] = jnp.concatenate(rows, axis=0)

    @pl.when(step == pl.num_programs(0) - 1)
    def _():
        tables = slot_tables(tile_ref)
        write_parts(parts_ref, to_slots(tables, adjoint_ref[...]))
        listed = listed_columns(tables, column_ref)
        for tile in range(TX):
            parts_ref[tile, pl.ds(LISTED, 8), :] = jnp.broadcast_to(listed[tile : tile + 1], (8, 128))


def middle_kernel(
    count_ref, tile_ref, weight_ref, returned_ref, earlier_ref, sums_in_ref, operator_ref,
    parts_ref, adjoint_ref, sums_ref, columns_ref, segments_ref,
):
    step = pl.program_id(0)

    @pl.when(step == 0)
    def _():
        columns_ref[...] = live_columns(count_ref, weight_ref[...])
        segments_ref[...] = from_slots(slot_tables(tile_ref), returned_ref[...])

    columns = group_columns(columns_ref, step)
    here = pl.ds(pl.multiple_of(step * GROUP, GROUP), GROUP)
    segments = segments_ref[here, :]
    rows = []
    for k in range(GROUP):
        block = operator_ref[k]
        observed = jnp.sum(block * segments[k : k + 1], axis=1, keepdims=True)
        rows.append(jnp.sum(block * (observed * columns[:, k : k + 1]), axis=0, keepdims=True))
    adjoint_ref[here, :] = jnp.concatenate(rows, axis=0)

    @pl.when(step == pl.num_programs(0) - 1)
    def _():
        adjoint = adjoint_ref[...]
        segments = segments_ref[...]
        write_parts(parts_ref, to_slots(slot_tables(tile_ref), adjoint))
        known = jnp.sum(earlier_ref[...] * segments, axis=0, keepdims=True)
        new = jnp.sum(adjoint * segments, axis=0, keepdims=True)
        sums = jnp.concatenate([sums_in_ref[2:4], known, new, jnp.zeros((4, 128), F32)], axis=0)
        sums_ref[...] = sums
        for tile in range(TX):
            parts_ref[tile, pl.ds(LISTED, 8), :] = sums
        adjoint_ref[...] = adjoint + earlier_ref[...]


def whole(shape):
    return pl.BlockSpec(shape, lambda i: (0,) * len(shape))


SCALARS = pl.BlockSpec(memory_space=pltpu.SMEM)
OPERATORS = pl.BlockSpec((GROUP, 128, 128), lambda i: (i, 0, 0))
PARTS = jax.ShapeDtypeStruct((TX, PART, 128), F32)
SQUARE = jax.ShapeDtypeStruct((OWN, 128), F32)
SUMS = jax.ShapeDtypeStruct((8, 128), F32)


def run_first(counts, tile, column, innovation, weight, operator):
    return pl.pallas_call(
        first_kernel,
        grid=(OWN // GROUP,),
        in_specs=[
            SCALARS, whole((1, OWN)), whole((1, OWN)), whole((OWN, 128)), whole((OWN, 128)), OPERATORS,
        ],
        out_specs=[whole((TX, PART, 128)), whole((OWN, 128))],
        out_shape=[PARTS, SQUARE],
        scratch_shapes=[pltpu.VMEM((OWN, OWN), F32)],
        cost_estimate=pl.CostEstimate(flops=4 * 128**3, bytes_accessed=9 << 20, transcendentals=0),
        name="first_adjoint",
    )(counts, tile, column, innovation, weight, operator)


def run_middle(counts, tile, weight, returned, earlier, sums, operator):
    return pl.pallas_call(
        middle_kernel,
        grid=(OWN // GROUP,),
        in_specs=[
            SCALARS, whole((1, OWN)), whole((OWN, 128)), whole((SLOTS, 128)), whole((OWN, 128)),
            whole((8, 128)), OPERATORS,
        ],
        out_specs=[whole((TX, PART, 128)), whole((OWN, 128)), whole((8, 128))],
        out_shape=[PARTS, SQUARE, SUMS],
        scratch_shapes=[pltpu.VMEM((OWN, OWN), F32), pltpu.VMEM((OWN, 128), F32)],
        cost_estimate=pl.CostEstimate(flops=8 * 128**3, bytes_accessed=10 << 20, transcendentals=0),
        name="observe",
    )(counts, tile, weight, returned, earlier, sums, operator)


def scatter(parts_ref, listed):
    column = listed.astype(jnp.int32)
    level = column >> 6
    cell = column & (CX - 1)
    lane = iota((TX, 128), 1)
    left = lane < CAP
    right = lane >= 2 * CAP
    place = jnp.where(left, cell - (CX - SIDE), jnp.where(right, cell + CX + SIDE, cell + SIDE))
    good = (lane < LISTED) & (place >= 0) & (place < EXT)
    row = jnp.where(good, level * EXT + place, -1)
    turned = pltpu.roll(row, PART, 1)
    one = jnp.where(lane < PART, row, turned)
    two = jnp.where(
        lane < 2 * PART - 128,
        turned,
        jnp.where(lane < 3 * PART - 128, pltpu.roll(row, 2 * PART - 128, 1), -1),
    )
    triple = jnp.concatenate([one, two], axis=1)
    down = iota((ROWS, 256), 0)
    total = jnp.zeros((ROWS, 128), F32)
    blank = jnp.zeros((256 - 3 * PART, 128), BF16)
    for source in range(TX):
        onehot = as_onehot(down == triple[source : source + 1])
        stacked = jnp.concatenate([*thirds(parts_ref[source]), blank], axis=0)
        total = total + jnp.dot(onehot, stacked, preferred_element_type=F32)
    return total


def edges(field, even):
    lane = iota((EXT, 128), 1)
    west = jnp.zeros((EXT, 128), F32)
    east = jnp.zeros((EXT, 128), F32)
    for level in range(LEV):
        part = field[level * EXT : (level + 1) * EXT]
        here = (lane >= 32 * level) & (lane < 32 * level + HALO)
        low = pltpu.roll(part, 32 * level, 1) if level else part
        west = jnp.where(here, low, west)
        east = jnp.where(here, pltpu.roll(part, (32 * level + HALO) % 128, 1), east)
    return jnp.where(even, east, west), jnp.where(even, west, east)


def parity(axis):
    return lax.axis_index(axis) % 2 == 0


def open_kernel(
    where_ref, parts_ref, sigma_ref, mask_ref, diffusivity_ref, near_ref, far_ref,
    field_ref, sigma_ext_ref, kappa_ext_ref, pair_ref, other_ref, listed_ref,
):
    row_no = where_ref[0]
    even_row = row_no % 2 == 0
    even = where_ref[1] % 2 == 0
    not_first = jnp.where(row_no > 0, 1.0, 0.0)
    not_last = jnp.where(row_no < TX - 1, 1.0, 0.0)
    for level in range(LEV):
        base = level * EXT
        near_k, far_k = near_ref[0, level], far_ref[0, level]
        near_s, far_s = near_ref[1, level], far_ref[1, level]
        kappa_ext_ref[pl.ds(base, SIDE), :] = jnp.where(even_row, far_k, near_k) * not_first
        kappa_ext_ref[pl.ds(base + SIDE, CX), :] = diffusivity_ref[level] * mask_ref[level].astype(F32)
        kappa_ext_ref[pl.ds(base + SIDE + CX, SIDE), :] = jnp.where(even_row, near_k, far_k) * not_last
        sigma_ext_ref[pl.ds(base, SIDE), :] = jnp.where(even_row, far_s, near_s)
        sigma_ext_ref[pl.ds(base + SIDE, CX), :] = sigma_ref[level]
        sigma_ext_ref[pl.ds(base + SIDE + CX, SIDE), :] = jnp.where(even_row, near_s, far_s)
    sigma_ext_ref[...] = jnp.where(kappa_ext_ref[...] > 0.0, sigma_ext_ref[...], 0.0)
    listed = jnp.concatenate([parts_ref[k, pl.ds(LISTED, 1), :] for k in range(TX)], axis=0)
    listed_ref[...] = listed
    field = scatter(parts_ref, listed) * sigma_ext_ref[...]
    field_ref[...] = field
    pair_ref[0], other_ref[0] = edges(field, even)
    pair_ref[1], other_ref[1] = edges(kappa_ext_ref[...], even)


def gather_kernel(where_ref, parts_ref, sigma_ext_ref, listed_ref, field_ref, pair_ref, other_ref):
    field = scatter(parts_ref, listed_ref[...]) * sigma_ext_ref[...]
    field_ref[...] = field
    pair_ref[0], other_ref[0] = edges(field, where_ref[1] % 2 == 0)


FIRST_ROW = SIDE - NSTEP - 6


def last_gather_kernel(where_ref, parts_ref, sigma_ext_ref, listed_ref, field_ref, message_ref):
    field = scatter(parts_ref, listed_ref[...]) * sigma_ext_ref[...]
    field_ref[...] = field
    lane = iota((STRIP, 128), 1)
    west = jnp.zeros((STRIP, 128), F32)
    east = jnp.zeros((STRIP, 128), F32)
    for level in range(LEV):
        for half in range(2):
            start = level * EXT + FIRST_ROW + half * STRIP
            part = field[start : start + STRIP]
            at = WIDE * (2 * level + half)
            here = (lane >= at) & (lane < at + NSTEP)
            west = jnp.where(here, pltpu.roll(part, at, 1) if at else part, west)
            east = jnp.where(here, pltpu.roll(part, (at + NSTEP) % 128, 1), east)
    sums = parts_ref[0, pl.ds(LISTED, 8), :]
    for source in range(1, TX):
        sums = sums + parts_ref[source, pl.ds(LISTED, 8), :]
    me = where_ref[1]
    for band in range(TY):
        message_ref[band, pl.ds(0, STRIP), :] = jnp.where(band == me + 1, east, west)
        message_ref[band, pl.ds(STRIP, 8), :] = sums


def widen(work_ref, field_ref, west_of, east_of, reach):
    lane = iota((EXT, 128), 1)
    for level in range(LEV):
        part = field_ref[pl.ds(level * EXT, EXT), :]
        first = jnp.where(
            (lane >= HALO - reach) & (lane < HALO), west_of(level), pltpu.roll(part, HALO, 1)
        )
        second = jnp.where(
            (lane >= 128 - HALO) & (lane < 128 - HALO + reach),
            east_of(level),
            pltpu.roll(part, 128 - HALO, 1),
        )
        work_ref[pl.ds(level, EXT, stride=8), :] = first
        work_ref[pl.ds(LEV + level, EXT, stride=8), :] = second


def tile_part(work_ref, level):
    lane = iota((CX, 128), 1)
    first = work_ref[pl.ds(SIDE * 8 + level, CX, stride=8), :]
    second = work_ref[pl.ds(SIDE * 8 + LEV + level, CX, stride=8), :]
    return jnp.where(lane < CY // 2, pltpu.roll(first, 128 - HALO, 1), pltpu.roll(second, HALO, 1))


def level_counts(count_ref):
    level = iota((8, 128), 0) % LEV
    counts = jnp.full((8, 128), count_ref[0], jnp.int32)
    for k in range(1, LEV):
        counts = jnp.where(level == k, count_ref[k], counts)
    return counts


def sweeps(work_ref, along_ref, across_ref, counts, first_row, end_row):
    def one(number, masked):
        active = counts > number
        flux = None
        now = work_ref[pl.ds(first_row * 8, 8), :]
        for row in range(first_row, end_row):
            here = pl.ds(row * 8, 8)
            side = across_ref[here, :] * (pltpu.roll(now, 127, 1) - now)
            change = side - pltpu.roll(side, 1, 1)
            if flux is not None:
                change = change - flux
            after = None
            if row + 1 < end_row:
                after = work_ref[pl.ds((row + 1) * 8, 8), :]
                flux = along_ref[here, :] * (after - now)
                change = change + flux
            if masked:
                change = jnp.where(active, change, 0.0)
            work_ref[here, :] = now + change
            now = after

    lax.fori_loop(0, MIN_STEPS, lambda n, c: (one(n, False), c)[1], 0)
    lax.fori_loop(MIN_STEPS, NSTEP, lambda n, c: (one(n, True), c)[1], 0)


def faces(work_ref, along_ref, across_ref):
    def mask_of(kappa):
        return jnp.where(kappa > 0.0, 1.0, 0.0)

    for row in range(EXT):
        here = pl.ds(row * 8, 8)
        kappa = work_ref[here, :]
        mask = mask_of(kappa)
        if row + 1 < EXT:
            after = work_ref[pl.ds((row + 1) * 8, 8), :]
            along_ref[here, :] = 0.5 * (mask * after + kappa * mask_of(after))
        else:
            along_ref[here, :] = jnp.zeros((8, 128), F32)
        beside = pltpu.roll(kappa, 127, 1)
        across_ref[here, :] = 0.5 * (mask * beside + kappa * mask_of(beside))


def strips(packed):
    west, east = packed

    def west_of(level):
        return pltpu.roll(west, 128 - 32 * level, 1) if level else west

    def east_of(level):
        return pltpu.roll(east, (2 * 128 - HALO - 32 * level) % 128, 1)

    return west_of, east_of


def from_pairs(near_ref, far_ref, which, even):
    near, far = near_ref[which], far_ref[which]
    return jnp.where(even, far, near), jnp.where(even, near, far)


def send_segments(picked_ref, listed_ref, segments):
    listed = jnp.concatenate([listed_ref[...], jnp.zeros((128 - TX, 128), F32)], axis=0).T
    mine = listed[CAP : 2 * CAP].astype(jnp.int32)
    lane = iota((CAP, LEV * CX), 1)
    hits = [
        jnp.where(mine[:, source : source + 1] == lane, 1.0, 0.0) for source in range(TX)
    ]
    onehot = jnp.concatenate(hits, axis=0).astype(BF16)
    picked_ref[...] = pick(onehot, segments)


INNER = (SIDE - NSTEP, SIDE + CX + NSTEP)
OUTER = (SIDE - HALO, SIDE + CX + HALO)


def spread_first_kernel(
    where_ref, count_ref, field_ref, kappa_ext_ref, near_ref, far_ref, sigma_ref, listed_ref,
    picked_ref, once_ref, twice_ref, along_ref, across_ref, work_ref,
):
    band = where_ref[1]
    even = band % 2 == 0
    west, east = from_pairs(near_ref, far_ref, 1, even)
    west = west * jnp.where(band > 0, 1.0, 0.0)
    east = east * jnp.where(band < TY - 1, 1.0, 0.0)
    widen(work_ref, kappa_ext_ref, *strips((west, east)), HALO)
    faces(work_ref, along_ref, across_ref)
    widen(work_ref, field_ref, *strips(from_pairs(near_ref, far_ref, 0, even)), HALO)
    counts = level_counts(count_ref)
    sweeps(work_ref, along_ref, across_ref, counts, *OUTER)
    for level in range(LEV):
        once_ref[level] = tile_part(work_ref, level)
    sweeps(work_ref, along_ref, across_ref, counts, *INNER)
    parts = []
    for level in range(LEV):
        part = tile_part(work_ref, level)
        twice_ref[level] = part
        parts.append(part * sigma_ref[level])
    send_segments(picked_ref, listed_ref, jnp.concatenate(parts, axis=0))


def spread_next_kernel(
    where_ref, count_ref, field_ref, near_ref, far_ref, sigma_ref, listed_ref, along_ref, across_ref,
    once_ref, twice_ref,
    picked_ref, image_ref, work_ref,
):
    even = where_ref[1] % 2 == 0
    widen(work_ref, field_ref, *strips(from_pairs(near_ref, far_ref, 0, even)), HALO)
    counts = level_counts(count_ref)
    sweeps(work_ref, along_ref, across_ref, counts, *OUTER)
    for level in range(LEV):
        image_ref[level] = once_ref[level] + tile_part(work_ref, level)
    sweeps(work_ref, along_ref, across_ref, counts, *INNER)
    parts = []
    for level in range(LEV):
        parts.append((twice_ref[level] + tile_part(work_ref, level)) * sigma_ref[level])
    send_segments(picked_ref, listed_ref, jnp.concatenate(parts, axis=0))


def spread_last_kernel(
    where_ref, count_ref, field_ref, message_ref, along_ref, across_ref, start_ref, image_ref,
    control_ref, residual_ref, work_ref,
):
    band = where_ref[1]
    west = message_ref[jnp.maximum(band - 1, 0), pl.ds(0, STRIP), :]
    east = message_ref[jnp.minimum(band + 1, TY - 1), pl.ds(0, STRIP), :]
    blank = jnp.zeros((FIRST_ROW, 128), F32)

    def side_of(packed, shift):
        def of(level):
            halves = [
                pltpu.roll(packed, (2 * 128 + shift - WIDE * (2 * level + half)) % 128, 1)
                for half in range(2)
            ]
            return jnp.concatenate([blank, *halves, blank], axis=0)

        return of

    widen(work_ref, field_ref, side_of(west, HALO - NSTEP), side_of(east, 128 - HALO), NSTEP)
    counts = level_counts(count_ref)
    sweeps(work_ref, along_ref, across_ref, counts, *INNER)

    sums = message_ref[0, pl.ds(STRIP, 8), :]
    for source in range(1, TY):
        sums = sums + message_ref[source, pl.ds(STRIP, 8), :]
    sums = jnp.sum(sums, axis=1, keepdims=True)
    start_start = sums[0:1]
    start_image = sums[0:1] + sums[1:2]
    image_image = sums[2:3]
    image_second = sums[2:3] + sums[3:4]
    step = start_start / start_image
    norm = step * step * image_image - 2.0 * step * start_image + start_start
    ratio = norm / start_start
    next_next = start_image - 2.0 * step * image_image + step * step * image_second
    next_start = start_image - step * image_image
    curvature = next_next + 2.0 * ratio * next_start + ratio * ratio * start_image
    second = norm / curvature
    for level in range(LEV):
        start = start_ref[level]
        image = image_ref[level]
        twice = image + tile_part(work_ref, level)
        remainder = start - step * image
        direction = remainder + ratio * start
        curved = (1.0 + ratio) * image - step * twice
        control_ref[level] = step * start + second * direction
        residual_ref[level] = remainder - second * curved


WORK = [pltpu.VMEM((EXT * 8, 128), F32)]
TILE = jax.ShapeDtypeStruct((LEV, CX, CY), F32)
WIDENED = jax.ShapeDtypeStruct((ROWS, 128), F32)
LAID = jax.ShapeDtypeStruct((EXT * 8, 128), F32)
LISTS = jax.ShapeDtypeStruct((TX, 128), F32)
PICKED = jax.ShapeDtypeStruct((SLOTS, 128), F32)


def edge_shape(number):
    return jax.ShapeDtypeStruct((number, EXT, 128), F32)


def tile_call(kernel, out_shape, scalars, arrays, name, scratch=()):
    vmem = pl.BlockSpec(memory_space=pltpu.VMEM)
    return pl.pallas_call(
        kernel,
        in_specs=[SCALARS] * len(scalars) + [vmem] * len(arrays),
        out_specs=[vmem] * len(out_shape),
        out_shape=list(out_shape),
        scratch_shapes=list(scratch),
        compiler_params=pltpu.CompilerParams(vmem_limit_bytes=32 << 20),
        name=name,
    )(*scalars, *arrays)


def swap_neighbours(for_pair, for_other, axis):
    count = lax.axis_size(axis)
    pairs = [(i, i ^ 1) for i in range(count)]
    others = [(i, (i + (1 if i % 2 else -1)) % count) for i in range(count)]
    return lax.ppermute(for_pair, axis, pairs), lax.ppermute(for_other, axis, others)


def exchange(parts):
    return lax.all_to_all(parts, "tx", split_axis=0, concat_axis=0, tiled=True)


def body(
    innovation,
    obs_weight,
    obs_operator,
    block_tile,
    owner_counts,
    block_column,
    sea_mask,
    diffusivity,
    background_std,
    step_counts,
):
    where = jnp.stack([lax.axis_index("tx"), lax.axis_index("ty")]).astype(jnp.int32)
    tile = block_tile.reshape(1, OWN)
    column = block_column.reshape(1, OWN)

    masked = diffusivity * sea_mask.astype(F32)
    low = jnp.stack([masked[:, :SIDE], background_std[:, :SIDE]])
    high = jnp.stack([masked[:, CX - SIDE :], background_std[:, CX - SIDE :]])
    even = parity("tx")
    near_x, far_x = swap_neighbours(jnp.where(even, high, low), jnp.where(even, low, high), "tx")

    parts, adjoint = run_first(owner_counts, tile, column, innovation, obs_weight, obs_operator)
    parts = exchange(parts)
    field, sigma_ext, kappa_ext, pair, other, listed = tile_call(
        open_kernel,
        (WIDENED, WIDENED, WIDENED, edge_shape(2), edge_shape(2), LISTS),
        (where,),
        (parts, background_std, sea_mask, diffusivity, near_x, far_x),
        "open_tile",
    )
    near, far = swap_neighbours(pair, other, "ty")
    picked, once, twice, along, across = tile_call(
        spread_first_kernel,
        (PICKED, TILE, TILE, LAID, LAID),
        (where, step_counts),
        (field, kappa_ext, near, far, background_std, listed),
        "spread_first",
        WORK,
    )
    returned = exchange(picked.reshape(TX, CAP, 128)).reshape(SLOTS, 128)
    sums = jnp.zeros((8, 128), F32)
    parts, adjoint, sums = run_middle(
        owner_counts, tile, obs_weight, returned, adjoint, sums, obs_operator
    )
    parts = exchange(parts)
    field, pair, other = tile_call(
        gather_kernel,
        (WIDENED, edge_shape(1), edge_shape(1)),
        (where,),
        (parts, sigma_ext, listed),
        "gather_tile",
    )
    near, far = swap_neighbours(pair, other, "ty")
    picked, image = tile_call(
        spread_next_kernel,
        (PICKED, TILE),
        (where, step_counts),
        (field, near, far, background_std, listed, along, across, once, twice),
        "spread_next",
        WORK,
    )
    returned = exchange(picked.reshape(TX, CAP, 128)).reshape(SLOTS, 128)
    parts, adjoint, sums = run_middle(
        owner_counts, tile, obs_weight, returned, adjoint, sums, obs_operator
    )
    parts = exchange(parts)
    field, message = tile_call(
        last_gather_kernel,
        (WIDENED, jax.ShapeDtypeStruct((TY, LAST, 128), F32)),
        (where,),
        (parts, sigma_ext, listed),
        "gather_last",
    )
    message = lax.all_to_all(message, "ty", split_axis=0, concat_axis=0, tiled=True)
    control_field, residual = tile_call(
        spread_last_kernel,
        (TILE, TILE),
        (where, step_counts),
        (field, message, along, across, once, image),
        "spread_last",
        WORK,
    )
    return control_field, residual


def solution(mesh):
    placed = (
        P(("tx", "ty"), None),
        P(("tx", "ty"), None),
        P(("tx", "ty"), None, None),
        P(("tx", "ty"), None),
        P(("tx", "ty")),
        P(("tx", "ty")),
        P(None, "tx", "ty"),
        P(None, "tx", "ty"),
        P(None, "tx", "ty"),
        P(),
    )
    return jax.shard_map(
        body,
        mesh=mesh,
        in_specs=placed,
        out_specs=(P(None, "tx", "ty"), P(None, "tx", "ty")),
        check_vma=False,
    )
```

```python
import jax
import jax.numpy as jnp
from jax import lax
from jax.experimental import pallas as pl
from jax.experimental.pallas import tpu as pltpu
from jax.sharding import PartitionSpec as P

F32 = jnp.float32
BF16 = jnp.bfloat16

LEV = 4
CX = 64
CY = 128
NSTEP = 10
MIN_STEPS = 5
UNROLL = 5
HALO = 2 * NSTEP
SIDE = 24
EXT = CX + 2 * SIDE
ROWS = LEV * EXT
OWN = 128
TX = 16
TY = 8
CAP = 24
SLOTS = TX * CAP
LISTED = 3 * CAP
PART = 80
GROUP = 16
GROUPS = OWN // GROUP
WIDE = 16
STRIP = 48
LAST = STRIP + 8


def iota(shape, dim):
    return lax.broadcasted_iota(jnp.int32, shape, dim)


def thirds(values):
    high = values.astype(BF16)
    rest = values - high.astype(F32)
    middle = rest.astype(BF16)
    low = (rest - middle.astype(F32)).astype(BF16)
    return high, middle, low


def pick(onehot, values):
    high, middle, low = thirds(values)
    total = jnp.dot(onehot, high, preferred_element_type=F32)
    total = total + jnp.dot(onehot, middle, preferred_element_type=F32)
    return total + jnp.dot(onehot, low, preferred_element_type=F32)


def as_onehot(hit):
    return jnp.where(hit, 1.0, 0.0).astype(BF16)


def slot_tables(tile_ref):
    down = iota((OWN, OWN), 0)
    across = iota((OWN, OWN), 1)
    tile_row = tile_ref[...].astype(F32)
    spread = jnp.broadcast_to(tile_row, (OWN, OWN))
    tile_col = jnp.sum(jnp.where(down == across, spread, 0.0), axis=1, keepdims=True)
    same = spread == tile_col
    rank_row = jnp.sum(jnp.where(same & (down < across), 1.0, 0.0), axis=0, keepdims=True)
    rank_col = jnp.sum(jnp.where(same & (across < down), 1.0, 0.0), axis=1, keepdims=True)
    return tile_row, rank_row, tile_col, rank_col


def write_parts(parts_ref, slots):
    for tile in range(TX):
        for side in (-1, 0, 1):
            source = tile + side
            rows = pl.ds((side + 1) * CAP, CAP)
            if 0 <= source < TX:
                parts_ref[tile, rows, :] = slots[source * CAP : (source + 1) * CAP]
            else:
                parts_ref[tile, rows, :] = jnp.zeros((CAP, 128), F32)


def to_slots(tables, adjoint):
    tile_row, rank_row, _, _ = tables
    slot_row = (tile_row * CAP + rank_row).astype(jnp.int32)
    return pick(as_onehot(iota((SLOTS, OWN), 0) == slot_row), adjoint)


def from_slots(tables, returned):
    _, _, tile_col, rank_col = tables
    slot_col = (tile_col * CAP + rank_col).astype(jnp.int32)
    return pick(as_onehot(iota((OWN, SLOTS), 1) == slot_col), returned)


def listed_columns(tables, column_ref):
    tile_row, _, _, rank_col = tables
    column_row = column_ref[...].astype(F32)
    tile_no = iota((TX, OWN), 0).astype(F32)
    lane = iota((OWN, 128), 1)
    rank = rank_col.astype(jnp.int32)
    total = jnp.zeros((TX, 128), F32)
    for side in (-1, 0, 1):
        mine = jnp.where(tile_row == tile_no + side, column_row, 0.0).astype(BF16)
        place = as_onehot(rank + (side + 1) * CAP == lane)
        total = total + jnp.dot(mine, place, preferred_element_type=F32)
    return total


def live_columns(count_ref, weighted):
    return jnp.where(iota((OWN, OWN), 1) < count_ref[0], weighted.T, 0.0)


def group(number):
    return pl.ds(pl.multiple_of(number * GROUP, GROUP), GROUP)


def load_blocks(operator_ref, blocks_ref, arrived):
    return lambda number: pltpu.make_async_copy(
        operator_ref.at[group(number)], blocks_ref.at[group(number)], arrived.at[number]
    )


def start_all(copy_of):
    for number in range(GROUPS):
        copy_of(number).start()


def first_kernel(
    count_ref, tile_ref, column_ref, innovation_ref, weight_ref, operator_ref,
    parts_ref, adjoint_ref, blocks_ref, repeated_ref, arrived,
):
    copy_of = load_blocks(operator_ref, blocks_ref, arrived)
    start_all(copy_of)
    tables = slot_tables(tile_ref)
    listed = listed_columns(tables, column_ref)
    for tile in range(TX):
        parts_ref[tile, pl.ds(LISTED, 8), :] = jnp.broadcast_to(listed[tile : tile + 1], (8, 128))
    eye = as_onehot(iota((OWN, OWN), 0) == iota((OWN, OWN), 1))
    ones = jnp.ones((2 * OWN, 128), BF16)

    def one_group(number, carry):
        here = group(number)
        live = iota((GROUP, OWN), 0) + number * GROUP < count_ref[0]
        weighted = jnp.where(live, weight_ref[here, :] * innovation_ref[here, :], 0.0)
        high, middle, _ = thirds(weighted)
        diagonals = [
            jnp.concatenate([eye * high[k : k + 1], eye * middle[k : k + 1]], axis=1)
            for k in range(GROUP)
        ]
        repeated_ref[...] = jnp.dot(
            jnp.concatenate(diagonals, axis=0), ones, preferred_element_type=F32
        )
        copy_of(number).wait()
        rows = []
        for k in range(GROUP):
            column = repeated_ref[pl.ds(k * OWN, OWN), :]
            block = blocks_ref[number * GROUP + k]
            rows.append(jnp.sum(block * column, axis=0, keepdims=True))
        adjoint_ref[here, :] = jnp.concatenate(rows, axis=0)
        return carry

    lax.fori_loop(0, GROUPS, one_group, 0)
    write_parts(parts_ref, to_slots(tables, adjoint_ref[...]))


def turn_kernel(operator_ref, turned_ref, done_ref, blocks_ref, lanes_ref, arrived, left):
    done_ref[...] = jnp.zeros((8, 128), F32)

    def copy_of(number):
        return pltpu.make_async_copy(
            operator_ref.at[:, group(number), :], blocks_ref.at[number], arrived.at[number]
        )

    def back(number):
        return pltpu.make_async_copy(
            lanes_ref.at[group(number)], turned_ref.at[group(number)], left.at[number]
        )

    start_all(copy_of)

    def one_group(number, carry):
        copy_of(number).wait()
        for k in range(GROUP):
            lanes_ref[number * GROUP + k] = blocks_ref[number, :, k, :].T
        back(number).start()
        return carry

    lax.fori_loop(0, GROUPS, one_group, 0)
    for number in range(GROUPS):
        back(number).wait()


def middle_kernel(
    count_ref, tile_ref, weight_ref, returned_ref, earlier_ref, turned_ref, *refs
):
    *sums_in_ref, parts_ref, adjoint_ref, sums_ref, weight_scr = refs
    tables = slot_tables(tile_ref)
    weight_scr[...] = live_columns(count_ref, weight_ref[...])
    own_segments = from_slots(tables, returned_ref[...])
    segments = own_segments.T

    def one_group(number, total):
        weight = weight_scr[group(number), :]
        for k in range(GROUP):
            block = turned_ref[number * GROUP + k]
            observed = jnp.sum(block * segments, axis=0, keepdims=True)
            total = total + block * (observed * weight[k : k + 1])
        return total

    total = lax.fori_loop(0, GROUPS, one_group, jnp.zeros((OWN, OWN), F32))
    adjoint = total.T
    write_parts(parts_ref, to_slots(tables, adjoint))
    known = jnp.sum(earlier_ref[...] * own_segments, axis=0, keepdims=True)
    new = jnp.sum(adjoint * own_segments, axis=0, keepdims=True)
    before = sums_in_ref[0][2:4] if sums_in_ref else jnp.zeros((2, 128), F32)
    sums = jnp.concatenate([before, known, new, jnp.zeros((4, 128), F32)], axis=0)
    sums_ref[...] = sums
    for tile in range(TX):
        parts_ref[tile, pl.ds(LISTED, 8), :] = sums
    adjoint_ref[...] = adjoint + earlier_ref[...]


VMEM_FIRST = 57 << 20
VMEM_TURN = 57 << 20
VMEM_OBSERVE = 16 << 20
SCALARS = pl.BlockSpec(memory_space=pltpu.SMEM)
HERE = pl.BlockSpec(memory_space=pltpu.VMEM)
THERE = pl.BlockSpec(memory_space=pltpu.HBM)
CUBE = (OWN, 128, 128)
PARTS = jax.ShapeDtypeStruct((TX, PART, 128), F32)
SQUARE = jax.ShapeDtypeStruct((OWN, 128), F32)
SUMS = jax.ShapeDtypeStruct((8, 128), F32)


def run_first(counts, tile, column, innovation, weight, operator):
    return pl.pallas_call(
        first_kernel,
        in_specs=[SCALARS, HERE, HERE, HERE, HERE, THERE],
        out_specs=[HERE, HERE],
        out_shape=[PARTS, SQUARE],
        scratch_shapes=[
            pltpu.VMEM(CUBE, F32),
            pltpu.VMEM((GROUP * OWN, 128), F32),
            pltpu.SemaphoreType.DMA((GROUPS,)),
        ],
        compiler_params=pltpu.CompilerParams(vmem_limit_bytes=VMEM_FIRST),
        cost_estimate=pl.CostEstimate(flops=4 * 128**3, bytes_accessed=9 << 20, transcendentals=0),
        name="first_adjoint",
    )(counts, tile, column, innovation, weight, operator)


def run_turn(operator):
    return pl.pallas_call(
        turn_kernel,
        in_specs=[THERE],
        out_specs=[THERE, HERE],
        out_shape=[jax.ShapeDtypeStruct(CUBE, F32), SUMS],
        scratch_shapes=[
            pltpu.VMEM((GROUPS, OWN, GROUP, 128), F32),
            pltpu.VMEM(CUBE, F32),
            pltpu.SemaphoreType.DMA((GROUPS,)),
            pltpu.SemaphoreType.DMA((GROUPS,)),
        ],
        compiler_params=pltpu.CompilerParams(vmem_limit_bytes=VMEM_TURN),
        cost_estimate=pl.CostEstimate(flops=0, bytes_accessed=16 << 20, transcendentals=0),
        name="blocks_on_lanes",
    )(operator)


def run_middle(counts, tile, weight, returned, earlier, turned, *sums):
    return pl.pallas_call(
        middle_kernel,
        in_specs=[SCALARS] + [HERE] * (5 + len(sums)),
        out_specs=[HERE, HERE, HERE],
        out_shape=[PARTS, SQUARE, SUMS],
        scratch_shapes=[pltpu.VMEM((OWN, OWN), F32)],
        compiler_params=pltpu.CompilerParams(vmem_limit_bytes=VMEM_OBSERVE),
        cost_estimate=pl.CostEstimate(flops=8 * 128**3, bytes_accessed=10 << 20, transcendentals=0),
        name="observe",
    )(counts, tile, weight, returned, earlier, turned, *sums)


def scatter(parts_ref, listed):
    column = listed.astype(jnp.int32)
    level = column >> 6
    cell = column & (CX - 1)
    lane = iota((TX, 128), 1)
    left = lane < CAP
    right = lane >= 2 * CAP
    place = jnp.where(left, cell - (CX - SIDE), jnp.where(right, cell + CX + SIDE, cell + SIDE))
    good = (lane < LISTED) & (place >= 0) & (place < EXT)
    row = jnp.where(good, level * EXT + place, -1)
    turned = pltpu.roll(row, PART, 1)
    one = jnp.where(lane < PART, row, turned)
    two = jnp.where(
        lane < 2 * PART - 128,
        turned,
        jnp.where(lane < 3 * PART - 128, pltpu.roll(row, 2 * PART - 128, 1), -1),
    )
    triple = jnp.concatenate([one, two], axis=1)
    down = iota((ROWS, 256), 0)
    total = jnp.zeros((ROWS, 128), F32)
    blank = jnp.zeros((256 - 3 * PART, 128), BF16)
    for source in range(TX):
        onehot = as_onehot(down == triple[source : source + 1])
        stacked = jnp.concatenate([*thirds(parts_ref[source]), blank], axis=0)
        total = total + jnp.dot(onehot, stacked, preferred_element_type=F32)
    return total


def edges(field, even):
    lane = iota((EXT, 128), 1)
    west = jnp.zeros((EXT, 128), F32)
    east = jnp.zeros((EXT, 128), F32)
    for level in range(LEV):
        part = field[level * EXT : (level + 1) * EXT]
        here = (lane >= 32 * level) & (lane < 32 * level + HALO)
        low = pltpu.roll(part, 32 * level, 1) if level else part
        west = jnp.where(here, low, west)
        east = jnp.where(here, pltpu.roll(part, (32 * level + HALO) % 128, 1), east)
    return jnp.where(even, east, west), jnp.where(even, west, east)


def parity(axis):
    return lax.axis_index(axis) % 2 == 0


def open_kernel(
    where_ref, parts_ref, sigma_ref, mask_ref, diffusivity_ref, near_ref, far_ref, _,
    field_ref, sigma_ext_ref, kappa_ext_ref, pair_ref, other_ref, listed_ref,
):
    row_no = where_ref[0]
    even_row = row_no % 2 == 0
    even = where_ref[1] % 2 == 0
    not_first = jnp.where(row_no > 0, 1.0, 0.0)
    not_last = jnp.where(row_no < TX - 1, 1.0, 0.0)
    for level in range(LEV):
        base = level * EXT
        near_k, far_k = near_ref[0, level], far_ref[0, level]
        near_s, far_s = near_ref[1, level], far_ref[1, level]
        kappa_ext_ref[pl.ds(base, SIDE), :] = jnp.where(even_row, far_k, near_k) * not_first
        kappa_ext_ref[pl.ds(base + SIDE, CX), :] = diffusivity_ref[level] * mask_ref[level].astype(F32)
        kappa_ext_ref[pl.ds(base + SIDE + CX, SIDE), :] = jnp.where(even_row, near_k, far_k) * not_last
        sigma_ext_ref[pl.ds(base, SIDE), :] = jnp.where(even_row, far_s, near_s)
        sigma_ext_ref[pl.ds(base + SIDE, CX), :] = sigma_ref[level]
        sigma_ext_ref[pl.ds(base + SIDE + CX, SIDE), :] = jnp.where(even_row, near_s, far_s)
    sigma_ext_ref[...] = jnp.where(kappa_ext_ref[...] > 0.0, sigma_ext_ref[...], 0.0)
    listed = jnp.concatenate([parts_ref[k, pl.ds(LISTED, 1), :] for k in range(TX)], axis=0)
    listed_ref[...] = listed
    field = scatter(parts_ref, listed) * sigma_ext_ref[...]
    field_ref[...] = field
    pair_ref[0], other_ref[0] = edges(field, even)
    pair_ref[1], other_ref[1] = edges(kappa_ext_ref[...], even)


def bring_kernel(listed_ref, _, brought_ref):
    brought_ref[...] = listed_ref[:8]


def gather_kernel(where_ref, parts_ref, sigma_ext_ref, listed_ref, field_ref, pair_ref, other_ref):
    field = scatter(parts_ref, listed_ref[...]) * sigma_ext_ref[...]
    field_ref[...] = field
    pair_ref[0], other_ref[0] = edges(field, where_ref[1] % 2 == 0)


FIRST_ROW = SIDE - NSTEP - 6


def last_gather_kernel(where_ref, parts_ref, sigma_ext_ref, listed_ref, field_ref, message_ref):
    field = scatter(parts_ref, listed_ref[...]) * sigma_ext_ref[...]
    field_ref[...] = field
    lane = iota((STRIP, 128), 1)
    west = jnp.zeros((STRIP, 128), F32)
    east = jnp.zeros((STRIP, 128), F32)
    for level in range(LEV):
        for half in range(2):
            start = level * EXT + FIRST_ROW + half * STRIP
            part = field[start : start + STRIP]
            at = WIDE * (2 * level + half)
            here = (lane >= at) & (lane < at + NSTEP)
            west = jnp.where(here, pltpu.roll(part, at, 1) if at else part, west)
            east = jnp.where(here, pltpu.roll(part, (at + NSTEP) % 128, 1), east)
    sums = parts_ref[0, pl.ds(LISTED, 8), :]
    for source in range(1, TX):
        sums = sums + parts_ref[source, pl.ds(LISTED, 8), :]
    me = where_ref[1]
    for band in range(TY):
        message_ref[band, pl.ds(0, STRIP), :] = jnp.where(band == me + 1, east, west)
        message_ref[band, pl.ds(STRIP, 8), :] = sums


def widen(work_ref, field_ref, west_of, east_of, reach):
    lane = iota((EXT, 128), 1)
    for level in range(LEV):
        part = field_ref[pl.ds(level * EXT, EXT), :]
        first = jnp.where(
            (lane >= HALO - reach) & (lane < HALO), west_of(level), pltpu.roll(part, HALO, 1)
        )
        second = jnp.where(
            (lane >= 128 - HALO) & (lane < 128 - HALO + reach),
            east_of(level),
            pltpu.roll(part, 128 - HALO, 1),
        )
        work_ref[pl.ds(level, EXT, stride=8), :] = first
        work_ref[pl.ds(LEV + level, EXT, stride=8), :] = second


def tile_part(work_ref, level):
    lane = iota((CX, 128), 1)
    first = work_ref[pl.ds(SIDE * 8 + level, CX, stride=8), :]
    second = work_ref[pl.ds(SIDE * 8 + LEV + level, CX, stride=8), :]
    return jnp.where(lane < CY // 2, pltpu.roll(first, 128 - HALO, 1), pltpu.roll(second, HALO, 1))


def level_counts(count_ref):
    level = iota((8, 128), 0) % LEV
    counts = jnp.full((8, 128), count_ref[0], jnp.int32)
    for k in range(1, LEV):
        counts = jnp.where(level == k, count_ref[k], counts)
    return counts


def sweeps(work_ref, along_ref, across_ref, counts, first_row, end_row):
    def one(number, masked):
        active = counts > number
        flux = None
        now = work_ref[pl.ds(first_row * 8, 8), :]
        for row in range(first_row, end_row):
            here = pl.ds(row * 8, 8)
            side = across_ref[here, :] * (pltpu.roll(now, 127, 1) - now)
            change = side - pltpu.roll(side, 1, 1)
            if flux is not None:
                change = change - flux
            after = None
            if row + 1 < end_row:
                after = work_ref[pl.ds((row + 1) * 8, 8), :]
                flux = along_ref[here, :] * (after - now)
                change = change + flux
            if masked:
                change = jnp.where(active, change, 0.0)
            work_ref[here, :] = now + change
            now = after

    def run(start, end, masked):
        def body(index, carry):
            for k in range(UNROLL):
                one(start + index * UNROLL + k, masked)
            return carry

        lax.fori_loop(0, (end - start) // UNROLL, body, 0)

    run(0, MIN_STEPS, False)
    run(MIN_STEPS, NSTEP, True)


def faces(work_ref, along_ref, across_ref):
    def mask_of(kappa):
        return jnp.where(kappa > 0.0, 1.0, 0.0)

    for row in range(EXT):
        here = pl.ds(row * 8, 8)
        kappa = work_ref[here, :]
        mask = mask_of(kappa)
        if row + 1 < EXT:
            after = work_ref[pl.ds((row + 1) * 8, 8), :]
            along_ref[here, :] = 0.5 * (mask * after + kappa * mask_of(after))
        else:
            along_ref[here, :] = jnp.zeros((8, 128), F32)
        beside = pltpu.roll(kappa, 127, 1)
        across_ref[here, :] = 0.5 * (mask * beside + kappa * mask_of(beside))


def strips(packed):
    west, east = packed

    def west_of(level):
        return pltpu.roll(west, 128 - 32 * level, 1) if level else west

    def east_of(level):
        return pltpu.roll(east, (2 * 128 - HALO - 32 * level) % 128, 1)

    return west_of, east_of


def from_pairs(near_ref, far_ref, which, even):
    near, far = near_ref[which], far_ref[which]
    return jnp.where(even, far, near), jnp.where(even, near, far)


def send_segments(picked_ref, listed_ref, segments):
    listed = jnp.concatenate([listed_ref[...], jnp.zeros((128 - TX, 128), F32)], axis=0).T
    mine = listed[CAP : 2 * CAP].astype(jnp.int32)
    lane = iota((CAP, LEV * CX), 1)
    hits = [
        jnp.where(mine[:, source : source + 1] == lane, 1.0, 0.0) for source in range(TX)
    ]
    onehot = jnp.concatenate(hits, axis=0).astype(BF16)
    picked_ref[...] = pick(onehot, segments)


INNER = (SIDE - NSTEP, SIDE + CX + NSTEP)
OUTER = (SIDE - HALO, SIDE + CX + HALO)


def spread_first_kernel(
    where_ref, count_ref, field_ref, kappa_ext_ref, near_ref, far_ref, sigma_ref, listed_ref, _,
    picked_ref, once_ref, twice_ref, along_ref, across_ref, work_ref,
):
    band = where_ref[1]
    even = band % 2 == 0
    west, east = from_pairs(near_ref, far_ref, 1, even)
    west = west * jnp.where(band > 0, 1.0, 0.0)
    east = east * jnp.where(band < TY - 1, 1.0, 0.0)
    widen(work_ref, kappa_ext_ref, *strips((west, east)), HALO)
    faces(work_ref, along_ref, across_ref)
    widen(work_ref, field_ref, *strips(from_pairs(near_ref, far_ref, 0, even)), HALO)
    counts = level_counts(count_ref)
    sweeps(work_ref, along_ref, across_ref, counts, *OUTER)
    for level in range(LEV):
        once_ref[level] = tile_part(work_ref, level)
    sweeps(work_ref, along_ref, across_ref, counts, *INNER)
    parts = []
    for level in range(LEV):
        part = tile_part(work_ref, level)
        twice_ref[level] = part
        parts.append(part * sigma_ref[level])
    send_segments(picked_ref, listed_ref, jnp.concatenate(parts, axis=0))


def spread_next_kernel(
    where_ref, count_ref, field_ref, near_ref, far_ref, sigma_ref, listed_ref, along_ref, across_ref,
    once_ref, twice_ref,
    picked_ref, image_ref, work_ref,
):
    even = where_ref[1] % 2 == 0
    widen(work_ref, field_ref, *strips(from_pairs(near_ref, far_ref, 0, even)), HALO)
    counts = level_counts(count_ref)
    sweeps(work_ref, along_ref, across_ref, counts, *OUTER)
    for level in range(LEV):
        image_ref[level] = once_ref[level] + tile_part(work_ref, level)
    sweeps(work_ref, along_ref, across_ref, counts, *INNER)
    parts = []
    for level in range(LEV):
        parts.append((twice_ref[level] + tile_part(work_ref, level)) * sigma_ref[level])
    send_segments(picked_ref, listed_ref, jnp.concatenate(parts, axis=0))


def spread_last_kernel(
    where_ref, count_ref, field_ref, message_ref, along_ref, across_ref, start_ref, image_ref,
    control_ref, residual_ref, work_ref,
):
    band = where_ref[1]
    west = message_ref[jnp.maximum(band - 1, 0), pl.ds(0, STRIP), :]
    east = message_ref[jnp.minimum(band + 1, TY - 1), pl.ds(0, STRIP), :]
    blank = jnp.zeros((FIRST_ROW, 128), F32)

    def side_of(packed, shift):
        def of(level):
            halves = [
                pltpu.roll(packed, (2 * 128 + shift - WIDE * (2 * level + half)) % 128, 1)
                for half in range(2)
            ]
            return jnp.concatenate([blank, *halves, blank], axis=0)

        return of

    widen(work_ref, field_ref, side_of(west, HALO - NSTEP), side_of(east, 128 - HALO), NSTEP)
    counts = level_counts(count_ref)
    sweeps(work_ref, along_ref, across_ref, counts, *INNER)

    sums = message_ref[0, pl.ds(STRIP, 8), :]
    for source in range(1, TY):
        sums = sums + message_ref[source, pl.ds(STRIP, 8), :]
    sums = jnp.sum(sums, axis=1, keepdims=True)
    start_start = sums[0:1]
    start_image = sums[0:1] + sums[1:2]
    image_image = sums[2:3]
    image_second = sums[2:3] + sums[3:4]
    step = start_start / start_image
    norm = step * step * image_image - 2.0 * step * start_image + start_start
    ratio = norm / start_start
    next_next = start_image - 2.0 * step * image_image + step * step * image_second
    next_start = start_image - step * image_image
    curvature = next_next + 2.0 * ratio * next_start + ratio * ratio * start_image
    second = norm / curvature
    for level in range(LEV):
        start = start_ref[level]
        image = image_ref[level]
        twice = image + tile_part(work_ref, level)
        remainder = start - step * image
        direction = remainder + ratio * start
        curved = (1.0 + ratio) * image - step * twice
        control_ref[level] = step * start + second * direction
        residual_ref[level] = remainder - second * curved


WORK = [pltpu.VMEM((EXT * 8, 128), F32)]
TILE = jax.ShapeDtypeStruct((LEV, CX, CY), F32)
WIDENED = jax.ShapeDtypeStruct((ROWS, 128), F32)
LAID = jax.ShapeDtypeStruct((EXT * 8, 128), F32)
LISTS = jax.ShapeDtypeStruct((TX, 128), F32)
PICKED = jax.ShapeDtypeStruct((SLOTS, 128), F32)


def edge_shape(number):
    return jax.ShapeDtypeStruct((number, EXT, 128), F32)


def tile_call(kernel, out_shape, scalars, arrays, name, scratch=(), after=()):
    return pl.pallas_call(
        kernel,
        in_specs=[SCALARS] * len(scalars) + [HERE] * len(arrays) + [HERE] * len(after),
        out_specs=[HERE] * len(out_shape),
        out_shape=list(out_shape),
        scratch_shapes=list(scratch),
        compiler_params=pltpu.CompilerParams(vmem_limit_bytes=16 << 20),
        name=name,
    )(*scalars, *arrays, *after)


def swap_neighbours(for_pair, for_other, axis):
    count = lax.axis_size(axis)
    pairs = [(i, i ^ 1) for i in range(count)]
    others = [(i, (i + (1 if i % 2 else -1)) % count) for i in range(count)]
    return lax.ppermute(for_pair, axis, pairs), lax.ppermute(for_other, axis, others)


def exchange(parts):
    return lax.all_to_all(parts, "tx", split_axis=0, concat_axis=0, tiled=True)


def body(
    innovation,
    obs_weight,
    obs_operator,
    block_tile,
    owner_counts,
    block_column,
    sea_mask,
    diffusivity,
    background_std,
    step_counts,
):
    where = jnp.stack([lax.axis_index("tx"), lax.axis_index("ty")]).astype(jnp.int32)
    tile = block_tile.reshape(1, OWN)
    column = block_column.reshape(1, OWN)

    masked = diffusivity * sea_mask.astype(F32)
    low = jnp.stack([masked[:, :SIDE], background_std[:, :SIDE]])
    high = jnp.stack([masked[:, CX - SIDE :], background_std[:, CX - SIDE :]])
    even = parity("tx")
    near_x, far_x = swap_neighbours(jnp.where(even, high, low), jnp.where(even, low, high), "tx")

    parts, adjoint = run_first(owner_counts, tile, column, innovation, obs_weight, obs_operator)
    parts, near_x, far_x = lax.optimization_barrier((parts, near_x, far_x))
    turned, done = run_turn(obs_operator)
    parts = exchange(parts)
    field, sigma_ext, kappa_ext, pair, other, listed = tile_call(
        open_kernel,
        (WIDENED, WIDENED, WIDENED, edge_shape(2), edge_shape(2), LISTS),
        (where,),
        (parts, background_std, sea_mask, diffusivity, near_x, far_x),
        "open_tile",
        after=(done,),
    )
    near, far = swap_neighbours(pair, other, "ty")
    brought = tile_call(bring_kernel, (SUMS,), (), (listed, turned), "bring_blocks")
    picked, once, twice, along, across = tile_call(
        spread_first_kernel,
        (PICKED, TILE, TILE, LAID, LAID),
        (where, step_counts),
        (field, kappa_ext, near, far, background_std, listed),
        "spread_first",
        WORK,
        after=brought,
    )
    returned = exchange(picked.reshape(TX, CAP, 128)).reshape(SLOTS, 128)
    parts, adjoint, sums = run_middle(owner_counts, tile, obs_weight, returned, adjoint, turned)
    parts = exchange(parts)
    field, pair, other = tile_call(
        gather_kernel,
        (WIDENED, edge_shape(1), edge_shape(1)),
        (where,),
        (parts, sigma_ext, listed),
        "gather_tile",
    )
    near, far = swap_neighbours(pair, other, "ty")
    picked, image = tile_call(
        spread_next_kernel,
        (PICKED, TILE),
        (where, step_counts),
        (field, near, far, background_std, listed, along, across, once, twice),
        "spread_next",
        WORK,
    )
    returned = exchange(picked.reshape(TX, CAP, 128)).reshape(SLOTS, 128)
    parts, adjoint, sums = run_middle(
        owner_counts, tile, obs_weight, returned, adjoint, turned, sums
    )
    parts = exchange(parts)
    field, message = tile_call(
        last_gather_kernel,
        (WIDENED, jax.ShapeDtypeStruct((TY, LAST, 128), F32)),
        (where,),
        (parts, sigma_ext, listed),
        "gather_last",
    )
    message = lax.all_to_all(message, "ty", split_axis=0, concat_axis=0, tiled=True)
    control_field, residual = tile_call(
        spread_last_kernel,
        (TILE, TILE),
        (where, step_counts),
        (field, message, along, across, once, image),
        "spread_last",
        WORK,
    )
    return control_field, residual


def solution(mesh):
    placed = (
        P(("tx", "ty"), None),
        P(("tx", "ty"), None),
        P(("tx", "ty"), None, None),
        P(("tx", "ty"), None),
        P(("tx", "ty")),
        P(("tx", "ty")),
        P(None, "tx", "ty"),
        P(None, "tx", "ty"),
        P(None, "tx", "ty"),
        P(),
    )
    return jax.shard_map(
        body,
        mesh=mesh,
        in_specs=placed,
        out_specs=(P(None, "tx", "ty"), P(None, "tx", "ty")),
        check_vma=False,
    )
```

```python
import jax
import jax.numpy as jnp
from jax import lax
from jax.experimental import pallas as pl
from jax.experimental.pallas import tpu as pltpu
from jax.sharding import PartitionSpec as P

F32 = jnp.float32
BF16 = jnp.bfloat16

LEV = 4
CX = 64
CY = 128
NSTEP = 10
MIN_STEPS = 5
UNROLL = 5
HALO = 2 * NSTEP
SIDE = 24
EXT = CX + 2 * SIDE
ROWS = LEV * EXT
OWN = 128
TX = 16
TY = 8
CAP = 24
SLOTS = TX * CAP
LISTED = 3 * CAP
PART = 80
GROUP = 16
GROUPS = OWN // GROUP


def iota(shape, dim):
    return lax.broadcasted_iota(jnp.int32, shape, dim)


def pieces(values):
    high = values.astype(BF16)
    return high, (values - high.astype(F32)).astype(BF16)


def pick(onehot, values):
    high, low = pieces(values)
    total = jnp.dot(onehot, high, preferred_element_type=F32)
    return total + jnp.dot(onehot, low, preferred_element_type=F32)


def as_onehot(hit):
    return jnp.where(hit, 1.0, 0.0).astype(BF16)


def slot_tables(tile_ref):
    down = iota((OWN, OWN), 0)
    across = iota((OWN, OWN), 1)
    tile_row = tile_ref[...].astype(F32)
    spread = jnp.broadcast_to(tile_row, (OWN, OWN))
    tile_col = jnp.sum(jnp.where(down == across, spread, 0.0), axis=1, keepdims=True)
    same = spread == tile_col
    rank_row = jnp.sum(jnp.where(same & (down < across), 1.0, 0.0), axis=0, keepdims=True)
    rank_col = jnp.sum(jnp.where(same & (across < down), 1.0, 0.0), axis=1, keepdims=True)
    return tile_row, rank_row, tile_col, rank_col


def write_parts(parts_ref, slots):
    for tile in range(TX):
        for side in (-1, 0, 1):
            source = tile + side
            rows = pl.ds((side + 1) * CAP, CAP)
            if 0 <= source < TX:
                parts_ref[tile, rows, :] = slots[source * CAP : (source + 1) * CAP]
            else:
                parts_ref[tile, rows, :] = jnp.zeros((CAP, 128), F32)


def to_slots(tables, adjoint):
    tile_row, rank_row, _, _ = tables
    slot_row = (tile_row * CAP + rank_row).astype(jnp.int32)
    return pick(as_onehot(iota((SLOTS, OWN), 0) == slot_row), adjoint)


def from_slots(tables, returned):
    _, _, tile_col, rank_col = tables
    slot_col = (tile_col * CAP + rank_col).astype(jnp.int32)
    return pick(as_onehot(iota((OWN, SLOTS), 1) == slot_col), returned)


def listed_columns(tables, column_ref):
    tile_row, _, _, rank_col = tables
    column_row = column_ref[...].astype(F32)
    tile_no = iota((TX, OWN), 0).astype(F32)
    lane = iota((OWN, 128), 1)
    rank = rank_col.astype(jnp.int32)
    total = jnp.zeros((TX, 128), F32)
    for side in (-1, 0, 1):
        mine = jnp.where(tile_row == tile_no + side, column_row, 0.0).astype(BF16)
        place = as_onehot(rank + (side + 1) * CAP == lane)
        total = total + jnp.dot(mine, place, preferred_element_type=F32)
    return total


def live_columns(count_ref, weighted):
    return jnp.where(iota((OWN, OWN), 1) < count_ref[0], weighted.T, 0.0)


def group(number):
    return pl.ds(pl.multiple_of(number * GROUP, GROUP), GROUP)


def load_blocks(operator_ref, blocks_ref, arrived):
    return lambda number: pltpu.make_async_copy(
        operator_ref.at[group(number)], blocks_ref.at[group(number)], arrived.at[number]
    )


def start_all(copy_of):
    for number in range(GROUPS):
        copy_of(number).start()


def first_kernel(
    count_ref, tile_ref, column_ref, innovation_ref, weight_ref, operator_ref,
    parts_ref, adjoint_ref, blocks_ref, arrived,
):
    copy_of = load_blocks(operator_ref, blocks_ref, arrived)
    start_all(copy_of)
    tables = slot_tables(tile_ref)
    listed = listed_columns(tables, column_ref)
    for tile in range(TX):
        parts_ref[tile, pl.ds(LISTED, 8), :] = jnp.broadcast_to(listed[tile : tile + 1], (8, 128))
    down = iota((8, 128), 0)

    def one_group(number, carry):
        here = group(number)
        live = iota((GROUP, OWN), 0) + number * GROUP < count_ref[0]
        weighted = jnp.where(live, weight_ref[here, :] * innovation_ref[here, :], 0.0)
        high = weighted.astype(BF16).astype(F32)
        low = weighted - high
        copy_of(number).wait()
        rows = []
        for k in range(GROUP):
            wide = jnp.broadcast_to(high[k : k + 1], (8, 128))
            narrow = jnp.broadcast_to(low[k : k + 1], (8, 128))
            first = jnp.where(down == 0, wide, 0.0)
            left = jnp.concatenate([jnp.where(down == 1, narrow, first), first], axis=1).astype(BF16)
            right = jnp.concatenate(pieces(blocks_ref[number * GROUP + k]), axis=0)
            product = jnp.dot(left, right, preferred_element_type=F32)
            rows.append(jnp.sum(product, axis=0, keepdims=True))
        adjoint_ref[here, :] = jnp.concatenate(rows, axis=0)
        return carry

    lax.fori_loop(0, GROUPS, one_group, 0)
    write_parts(parts_ref, to_slots(tables, adjoint_ref[...]))


def turn_kernel(operator_ref, turned_ref, done_ref, blocks_ref, lanes_ref, arrived, left):
    done_ref[...] = jnp.zeros((8, 128), F32)

    def copy_of(number):
        return pltpu.make_async_copy(
            operator_ref.at[:, group(number), :], blocks_ref.at[number], arrived.at[number]
        )

    def back(number):
        return pltpu.make_async_copy(
            lanes_ref.at[group(number)], turned_ref.at[group(number)], left.at[number]
        )

    start_all(copy_of)

    def one_group(number, carry):
        copy_of(number).wait()
        for k in range(GROUP):
            lanes_ref[number * GROUP + k] = blocks_ref[number, :, k, :].T
        back(number).start()
        return carry

    lax.fori_loop(0, GROUPS, one_group, 0)
    for number in range(GROUPS):
        back(number).wait()


def middle_kernel(
    count_ref, tile_ref, weight_ref, returned_ref, earlier_ref, turned_ref, *refs
):
    *sums_in_ref, parts_ref, adjoint_ref, sums_ref, weight_scr = refs
    tables = slot_tables(tile_ref)
    weight_scr[...] = live_columns(count_ref, weight_ref[...])
    own_segments = from_slots(tables, returned_ref[...])
    segments = own_segments.T

    def one_group(number, total):
        weight = weight_scr[group(number), :]
        for k in range(GROUP):
            block = turned_ref[number * GROUP + k]
            observed = jnp.sum(block * segments, axis=0, keepdims=True)
            total = total + block * (observed * weight[k : k + 1])
        return total

    total = lax.fori_loop(0, GROUPS, one_group, jnp.zeros((OWN, OWN), F32))
    adjoint = total.T
    write_parts(parts_ref, to_slots(tables, adjoint))
    known = jnp.sum(earlier_ref[...] * own_segments, axis=0, keepdims=True)
    new = jnp.sum(adjoint * own_segments, axis=0, keepdims=True)
    before = sums_in_ref[0][2:4] if sums_in_ref else jnp.zeros((2, 128), F32)
    sums = jnp.concatenate([before, known, new, jnp.zeros((4, 128), F32)], axis=0)
    sums_ref[...] = sums
    if sums_in_ref:
        for tile in range(TX):
            parts_ref[tile, pl.ds(LISTED, 8), :] = sums
    adjoint_ref[...] = adjoint + earlier_ref[...]


VMEM_FIRST = 57 << 20
VMEM_TURN = 57 << 20
VMEM_OBSERVE = 16 << 20
SCALARS = pl.BlockSpec(memory_space=pltpu.SMEM)
HERE = pl.BlockSpec(memory_space=pltpu.VMEM)
THERE = pl.BlockSpec(memory_space=pltpu.HBM)
CUBE = (OWN, 128, 128)
PLAIN_PARTS = jax.ShapeDtypeStruct((TX, LISTED, 128), F32)
PARTS = jax.ShapeDtypeStruct((TX, PART, 128), F32)
SQUARE = jax.ShapeDtypeStruct((OWN, 128), F32)
SUMS = jax.ShapeDtypeStruct((8, 128), F32)


def run_first(counts, tile, column, innovation, weight, operator):
    return pl.pallas_call(
        first_kernel,
        in_specs=[SCALARS, HERE, HERE, HERE, HERE, THERE],
        out_specs=[HERE, HERE],
        out_shape=[PARTS, SQUARE],
        scratch_shapes=[
            pltpu.VMEM(CUBE, F32),
            pltpu.SemaphoreType.DMA((GROUPS,)),
        ],
        compiler_params=pltpu.CompilerParams(vmem_limit_bytes=VMEM_FIRST),
        cost_estimate=pl.CostEstimate(flops=4 * 128**3, bytes_accessed=9 << 20, transcendentals=0),
        name="first_adjoint",
    )(counts, tile, column, innovation, weight, operator)


def run_turn(operator):
    return pl.pallas_call(
        turn_kernel,
        in_specs=[THERE],
        out_specs=[THERE, HERE],
        out_shape=[jax.ShapeDtypeStruct(CUBE, F32), SUMS],
        scratch_shapes=[
            pltpu.VMEM((GROUPS, OWN, GROUP, 128), F32),
            pltpu.VMEM(CUBE, F32),
            pltpu.SemaphoreType.DMA((GROUPS,)),
            pltpu.SemaphoreType.DMA((GROUPS,)),
        ],
        compiler_params=pltpu.CompilerParams(vmem_limit_bytes=VMEM_TURN),
        cost_estimate=pl.CostEstimate(flops=0, bytes_accessed=16 << 20, transcendentals=0),
        name="blocks_on_lanes",
    )(operator)


def run_middle(counts, tile, weight, returned, earlier, turned, *sums):
    return pl.pallas_call(
        middle_kernel,
        in_specs=[SCALARS] + [HERE] * (5 + len(sums)),
        out_specs=[HERE, HERE, HERE],
        out_shape=[PARTS if sums else PLAIN_PARTS, SQUARE, SUMS],
        scratch_shapes=[pltpu.VMEM((OWN, OWN), F32)],
        compiler_params=pltpu.CompilerParams(vmem_limit_bytes=VMEM_OBSERVE),
        cost_estimate=pl.CostEstimate(flops=8 * 128**3, bytes_accessed=10 << 20, transcendentals=0),
        name="observe",
    )(counts, tile, weight, returned, earlier, turned, *sums)


def flat_list(listed, part):
    lane = iota((1, 128), 1)
    words = [jnp.zeros((1, 128), F32)] * (SLOTS // 128)
    for source in range(TX):
        start = CAP * source
        turned = pltpu.roll(listed[source : source + 1], (start - CAP * part) % 128, 1)
        for word in range(start // 128, (start + CAP - 1) // 128 + 1):
            here = (lane + 128 * word >= start) & (lane + 128 * word < start + CAP)
            words[word] = jnp.where(here, turned, words[word])
    return jnp.concatenate(words, axis=1).astype(jnp.int32)


def target_rows(listed):
    west, own, east = (flat_list(listed, part) for part in range(3))
    cell = west & (CX - 1)
    west = jnp.where(cell >= CX - SIDE, (west >> 6) * SIDE + cell - (CX - SIDE), -1)
    cell = east & (CX - 1)
    east = jnp.where(cell < SIDE, (east >> 6) * SIDE + cell, -1)
    return jnp.concatenate([west, own, east, jnp.zeros((5, SLOTS), jnp.int32)], axis=0)


def scatter(field_ref, parts_ref, rows_ref, sigma_ext_ref):
    at = 0
    for part, width in ((0, SIDE), (1, CX), (2, SIDE)):
        values = jnp.concatenate(
            [parts_ref[source, pl.ds(part * CAP, CAP), :] for source in range(TX)], axis=0
        )
        onehot = as_onehot(iota((LEV * width, SLOTS), 0) == rows_ref[part : part + 1, :])
        total = jnp.dot(
            jnp.concatenate([onehot, onehot], axis=1),
            jnp.concatenate(pieces(values), axis=0),
            preferred_element_type=F32,
        )
        for level in range(LEV):
            here = pl.ds(level * EXT + at, width)
            field_ref[here, :] = total[level * width : (level + 1) * width] * sigma_ext_ref[here, :]
        at += width


def edges(field, even):
    lane = iota((EXT, 128), 1)
    west = jnp.zeros((EXT, 128), F32)
    east = jnp.zeros((EXT, 128), F32)
    for level in range(LEV):
        part = field[level * EXT : (level + 1) * EXT]
        here = (lane >= 32 * level) & (lane < 32 * level + HALO)
        low = pltpu.roll(part, 32 * level, 1) if level else part
        west = jnp.where(here, low, west)
        east = jnp.where(here, pltpu.roll(part, (32 * level + HALO) % 128, 1), east)
    return jnp.where(even, east, west), jnp.where(even, west, east)


def parity(axis):
    return lax.axis_index(axis) % 2 == 0


def prepare_kernel(mask_ref, diffusivity_ref, sigma_ref, kappa_ref, pair_ref, other_ref):
    even = parity("tx")
    for level in range(LEV):
        kappa = diffusivity_ref[level] * mask_ref[level].astype(F32)
        kappa_ref[level] = kappa
        for number, values in ((0, kappa), (1, sigma_ref[level])):
            low, high = values[:SIDE], values[CX - SIDE :]
            pair_ref[number, level] = jnp.where(even, high, low)
            other_ref[number, level] = jnp.where(even, low, high)


def open_kernel(
    parts_ref, sigma_ref, kappa_ref, near_ref, far_ref, _,
    field_ref, sigma_ext_ref, kappa_ext_ref, pair_ref, other_ref, listed_ref, rows_ref,
):
    row_no = lax.axis_index("tx")
    even_row = parity("tx")
    even = parity("ty")
    not_first = jnp.where(row_no > 0, 1.0, 0.0)
    not_last = jnp.where(row_no < TX - 1, 1.0, 0.0)
    for level in range(LEV):
        base = level * EXT
        near_k, far_k = near_ref[0, level], far_ref[0, level]
        near_s, far_s = near_ref[1, level], far_ref[1, level]
        kappa_ext_ref[pl.ds(base, SIDE), :] = jnp.where(even_row, far_k, near_k) * not_first
        kappa_ext_ref[pl.ds(base + SIDE, CX), :] = kappa_ref[level]
        kappa_ext_ref[pl.ds(base + SIDE + CX, SIDE), :] = jnp.where(even_row, near_k, far_k) * not_last
        sigma_ext_ref[pl.ds(base, SIDE), :] = jnp.where(even_row, far_s, near_s)
        sigma_ext_ref[pl.ds(base + SIDE, CX), :] = sigma_ref[level]
        sigma_ext_ref[pl.ds(base + SIDE + CX, SIDE), :] = jnp.where(even_row, near_s, far_s)
    sigma_ext_ref[...] = jnp.where(kappa_ext_ref[...] > 0.0, sigma_ext_ref[...], 0.0)
    listed = jnp.concatenate([parts_ref[k, pl.ds(LISTED, 1), :] for k in range(TX)], axis=0)
    listed_ref[...] = listed
    rows_ref[...] = target_rows(listed)
    scatter(field_ref, parts_ref, rows_ref, sigma_ext_ref)
    pair_ref[0], other_ref[0] = edges(field_ref[...], even)
    pair_ref[1], other_ref[1] = edges(kappa_ext_ref[...], even)


def bring_kernel(listed_ref, _, brought_ref):
    brought_ref[...] = listed_ref[:8]


def gather_kernel(parts_ref, sigma_ext_ref, rows_ref, field_ref, pair_ref, other_ref):
    scatter(field_ref, parts_ref, rows_ref, sigma_ext_ref)
    pair_ref[0], other_ref[0] = edges(field_ref[...], parity("ty"))


def last_gather_kernel(parts_ref, sigma_ext_ref, rows_ref, field_ref, pair_ref, other_ref, sums_ref):
    scatter(field_ref, parts_ref, rows_ref, sigma_ext_ref)
    pair_ref[0, pl.ds(0, EXT), :], other_ref[0, pl.ds(0, EXT), :] = edges(field_ref[...], parity("ty"))
    sums = parts_ref[0, pl.ds(LISTED, 8), :]
    for source in range(1, TX):
        sums = sums + parts_ref[source, pl.ds(LISTED, 8), :]
    pair_ref[0, pl.ds(EXT, 8), :] = sums
    other_ref[0, pl.ds(EXT, 8), :] = sums
    sums_ref[...] = sums


def meet_kernel(sums_ref, near_ref, far_ref, three_ref, two_ref):
    near, far = near_ref[0, pl.ds(EXT, 8), :], far_ref[0, pl.ds(EXT, 8), :]
    two_ref[...] = sums_ref[...] + jnp.where(parity("ty"), far, near)
    three_ref[...] = sums_ref[...] + near + far


def widen(work_ref, field_ref, west_of, east_of):
    lane = iota((EXT, 128), 1)
    for level in range(LEV):
        part = field_ref[pl.ds(level * EXT, EXT), :]
        first = jnp.where(
            lane < HALO, west_of(level), pltpu.roll(part, HALO, 1)
        )
        second = jnp.where(
            lane >= 128 - HALO,
            east_of(level),
            pltpu.roll(part, 128 - HALO, 1),
        )
        work_ref[pl.ds(level, EXT, stride=8), :] = first
        work_ref[pl.ds(LEV + level, EXT, stride=8), :] = second


def tile_part(work_ref, level):
    lane = iota((CX, 128), 1)
    first = work_ref[pl.ds(SIDE * 8 + level, CX, stride=8), :]
    second = work_ref[pl.ds(SIDE * 8 + LEV + level, CX, stride=8), :]
    return jnp.where(lane < CY // 2, pltpu.roll(first, 128 - HALO, 1), pltpu.roll(second, HALO, 1))


def level_counts(count_ref):
    level = iota((8, 128), 0) % LEV
    counts = jnp.full((8, 128), count_ref[0], jnp.int32)
    for k in range(1, LEV):
        counts = jnp.where(level == k, count_ref[k], counts)
    return counts


def sweeps(work_ref, along_ref, across_ref, counts, first_row, end_row):
    def one(number, masked, first_row, end_row):
        active = counts > number
        flux = None
        now = work_ref[pl.ds(first_row * 8, 8), :]
        for row in range(first_row, end_row):
            here = pl.ds(row * 8, 8)
            side = across_ref[here, :] * (pltpu.roll(now, 127, 1) - now)
            change = side - pltpu.roll(side, 1, 1)
            if flux is not None:
                change = change - flux
            after = None
            if row + 1 < end_row:
                after = work_ref[pl.ds((row + 1) * 8, 8), :]
                flux = along_ref[here, :] * (after - now)
                change = change + flux
            if masked:
                change = jnp.where(active, change, 0.0)
            work_ref[here, :] = now + change
            now = after

    def run(start, end, masked, *rows):
        def body(index, carry):
            for k in range(UNROLL):
                one(start + index * UNROLL + k, masked, *rows)
            return carry

        lax.fori_loop(0, (end - start) // UNROLL, body, 0)

    run(0, MIN_STEPS, False, first_row, end_row)
    run(MIN_STEPS, NSTEP, True, first_row + MIN_STEPS, end_row - MIN_STEPS)


def faces(work_ref, along_ref, across_ref):
    def mask_of(kappa):
        return jnp.where(kappa > 0.0, 1.0, 0.0)

    for row in range(EXT):
        here = pl.ds(row * 8, 8)
        kappa = work_ref[here, :]
        mask = mask_of(kappa)
        if row + 1 < EXT:
            after = work_ref[pl.ds((row + 1) * 8, 8), :]
            along_ref[here, :] = 0.5 * (mask * after + kappa * mask_of(after))
        else:
            along_ref[here, :] = jnp.zeros((8, 128), F32)
        beside = pltpu.roll(kappa, 127, 1)
        across_ref[here, :] = 0.5 * (mask * beside + kappa * mask_of(beside))


def strips(packed):
    west, east = packed

    def west_of(level):
        return pltpu.roll(west, 128 - 32 * level, 1) if level else west

    def east_of(level):
        return pltpu.roll(east, (2 * 128 - HALO - 32 * level) % 128, 1)

    return west_of, east_of


def from_pairs(near_ref, far_ref, which):
    near, far = near_ref[which, pl.ds(0, EXT), :], far_ref[which, pl.ds(0, EXT), :]
    even = parity("ty")
    return jnp.where(even, far, near), jnp.where(even, near, far)


def send_segments(picked_ref, listed_ref, segments):
    listed = jnp.concatenate([listed_ref[...], jnp.zeros((128 - TX, 128), F32)], axis=0).T
    mine = listed[CAP : 2 * CAP].astype(jnp.int32)
    lane = iota((CAP, LEV * CX), 1)
    hits = [
        jnp.where(mine[:, source : source + 1] == lane, 1.0, 0.0) for source in range(TX)
    ]
    onehot = jnp.concatenate(hits, axis=0).astype(BF16)
    picked_ref[...] = pick(onehot, segments)


INNER = (SIDE - NSTEP, SIDE + CX + NSTEP)
OUTER = (SIDE - HALO, SIDE + CX + HALO)


def spread_first_kernel(
    count_ref, field_ref, kappa_ext_ref, near_ref, far_ref, sigma_ref, listed_ref, _,
    picked_ref, once_ref, twice_ref, along_ref, across_ref, work_ref,
):
    band = lax.axis_index("ty")
    west, east = from_pairs(near_ref, far_ref, 1)
    west = west * jnp.where(band > 0, 1.0, 0.0)
    east = east * jnp.where(band < TY - 1, 1.0, 0.0)
    widen(work_ref, kappa_ext_ref, *strips((west, east)))
    faces(work_ref, along_ref, across_ref)
    widen(work_ref, field_ref, *strips(from_pairs(near_ref, far_ref, 0)))
    counts = level_counts(count_ref)
    sweeps(work_ref, along_ref, across_ref, counts, *OUTER)
    for level in range(LEV):
        once_ref[level] = tile_part(work_ref, level)
    sweeps(work_ref, along_ref, across_ref, counts, *INNER)
    parts = []
    for level in range(LEV):
        part = tile_part(work_ref, level)
        twice_ref[level] = part
        parts.append(part * sigma_ref[level])
    send_segments(picked_ref, listed_ref, jnp.concatenate(parts, axis=0))


def spread_next_kernel(
    count_ref, field_ref, near_ref, far_ref, sigma_ref, listed_ref, along_ref, across_ref,
    once_ref, twice_ref,
    picked_ref, image_ref, work_ref,
):
    widen(work_ref, field_ref, *strips(from_pairs(near_ref, far_ref, 0)))
    counts = level_counts(count_ref)
    sweeps(work_ref, along_ref, across_ref, counts, *OUTER)
    for level in range(LEV):
        image_ref[level] = once_ref[level] + tile_part(work_ref, level)
    sweeps(work_ref, along_ref, across_ref, counts, *INNER)
    parts = []
    for level in range(LEV):
        parts.append((twice_ref[level] + tile_part(work_ref, level)) * sigma_ref[level])
    send_segments(picked_ref, listed_ref, jnp.concatenate(parts, axis=0))


def spread_last_kernel(count_ref, field_ref, near_ref, far_ref, along_ref, across_ref, last_ref, work_ref):
    widen(work_ref, field_ref, *strips(from_pairs(near_ref, far_ref, 0)))
    sweeps(work_ref, along_ref, across_ref, level_counts(count_ref), *INNER)
    for level in range(LEV):
        last_ref[level] = tile_part(work_ref, level)


def finish_kernel(
    last_ref, three_ref, next_ref, previous_ref, start_ref, image_ref, control_ref, residual_ref
):
    sums = three_ref[...] + next_ref[...] + previous_ref[...]
    sums = jnp.sum(sums, axis=1, keepdims=True)
    start_start = sums[0:1]
    start_image = sums[0:1] + sums[1:2]
    image_image = sums[2:3]
    image_second = sums[2:3] + sums[3:4]
    step = start_start / start_image
    norm = step * step * image_image - 2.0 * step * start_image + start_start
    ratio = norm / start_start
    next_next = start_image - 2.0 * step * image_image + step * step * image_second
    next_start = start_image - step * image_image
    curvature = next_next + 2.0 * ratio * next_start + ratio * ratio * start_image
    second = norm / curvature
    for level in range(LEV):
        start = start_ref[level]
        image = image_ref[level]
        twice = image + last_ref[level]
        remainder = start - step * image
        direction = remainder + ratio * start
        curved = (1.0 + ratio) * image - step * twice
        control_ref[level] = step * start + second * direction
        residual_ref[level] = remainder - second * curved


WORK = [pltpu.VMEM((EXT * 8, 128), F32)]
TILE = jax.ShapeDtypeStruct((LEV, CX, CY), F32)
WIDENED = jax.ShapeDtypeStruct((ROWS, 128), F32)
LAID = jax.ShapeDtypeStruct((EXT * 8, 128), F32)
TARGETS = jax.ShapeDtypeStruct((8, SLOTS), jnp.int32)
LISTS = jax.ShapeDtypeStruct((TX, 128), F32)
PICKED = jax.ShapeDtypeStruct((SLOTS, 128), F32)


def edge_shape(number, more=0):
    return jax.ShapeDtypeStruct((number, EXT + more, 128), F32)


def tile_call(kernel, out_shape, scalars, arrays, name, scratch=(), after=()):
    return pl.pallas_call(
        kernel,
        in_specs=[SCALARS] * len(scalars) + [HERE] * len(arrays) + [HERE] * len(after),
        out_specs=[HERE] * len(out_shape),
        out_shape=list(out_shape),
        scratch_shapes=list(scratch),
        compiler_params=pltpu.CompilerParams(vmem_limit_bytes=16 << 20),
        name=name,
    )(*scalars, *arrays, *after)


def swap_neighbours(for_pair, for_other, axis):
    count = lax.axis_size(axis)
    pairs = [(i, i ^ 1) for i in range(count)]
    others = [(i, (i + (1 if i % 2 else -1)) % count) for i in range(count)]
    return lax.ppermute(for_pair, axis, pairs), lax.ppermute(for_other, axis, others)


def exchange(parts):
    return lax.all_to_all(parts, "tx", split_axis=0, concat_axis=0, tiled=True)


def body(
    innovation,
    obs_weight,
    obs_operator,
    block_tile,
    owner_counts,
    block_column,
    sea_mask,
    diffusivity,
    background_std,
    step_counts,
):
    tile = block_tile.reshape(1, OWN)
    column = block_column.reshape(1, OWN)

    rows_shape = jax.ShapeDtypeStruct((2, LEV, SIDE, 128), F32)
    kappa, pair, other = tile_call(
        prepare_kernel,
        (TILE, rows_shape, rows_shape),
        (),
        (sea_mask, diffusivity, background_std),
        "prepare",
    )
    near_x, far_x = swap_neighbours(pair, other, "tx")
    parts, adjoint = run_first(owner_counts, tile, column, innovation, obs_weight, obs_operator)
    turned, done = run_turn(obs_operator)
    parts = exchange(parts)
    field, sigma_ext, kappa_ext, pair, other, listed, rows = tile_call(
        open_kernel,
        (WIDENED, WIDENED, WIDENED, edge_shape(2), edge_shape(2), LISTS, TARGETS),
        (),
        (parts, background_std, kappa, near_x, far_x),
        "open_tile",
        after=(done,),
    )
    near, far = swap_neighbours(pair, other, "ty")
    brought = tile_call(bring_kernel, (SUMS,), (), (listed, turned), "bring_blocks")
    picked, once, twice, along, across = tile_call(
        spread_first_kernel,
        (PICKED, TILE, TILE, LAID, LAID),
        (step_counts,),
        (field, kappa_ext, near, far, background_std, listed),
        "spread_first",
        WORK,
        after=brought,
    )
    returned = exchange(picked.reshape(TX, CAP, 128)).reshape(SLOTS, 128)
    parts, adjoint, sums = run_middle(owner_counts, tile, obs_weight, returned, adjoint, turned)
    parts = exchange(parts)
    field, pair, other = tile_call(
        gather_kernel,
        (WIDENED, edge_shape(1), edge_shape(1)),
        (),
        (parts, sigma_ext, rows),
        "gather_tile",
    )
    near, far = swap_neighbours(pair, other, "ty")
    picked, image = tile_call(
        spread_next_kernel,
        (PICKED, TILE),
        (step_counts,),
        (field, near, far, background_std, listed, along, across, once, twice),
        "spread_next",
        WORK,
    )
    returned = exchange(picked.reshape(TX, CAP, 128)).reshape(SLOTS, 128)
    parts, adjoint, sums = run_middle(
        owner_counts, tile, obs_weight, returned, adjoint, turned, sums
    )
    parts = exchange(parts)
    field, pair, other, sums = tile_call(
        last_gather_kernel,
        (WIDENED, edge_shape(1, 8), edge_shape(1, 8), SUMS),
        (),
        (parts, sigma_ext, rows),
        "gather_last",
    )
    near, far = swap_neighbours(pair, other, "ty")
    three, two = tile_call(meet_kernel, (SUMS, SUMS), (), (sums, near, far), "meet")
    bands = lax.axis_size("ty")
    after = lax.ppermute(three, "ty", [(i, (i - 3) % bands) for i in range(bands)])
    before = lax.ppermute(two, "ty", [(i, (i + 2) % bands) for i in range(bands)])
    last = tile_call(
        spread_last_kernel,
        (TILE,),
        (step_counts,),
        (field, near, far, along, across),
        "spread_last",
        WORK,
    )[0]
    control_field, residual = tile_call(
        finish_kernel, (TILE, TILE), (), (last, three, after, before, once, image), "finish"
    )
    return control_field, residual


def solution(mesh):
    placed = (
        P(("tx", "ty"), None),
        P(("tx", "ty"), None),
        P(("tx", "ty"), None, None),
        P(("tx", "ty"), None),
        P(("tx", "ty")),
        P(("tx", "ty")),
        P(None, "tx", "ty"),
        P(None, "tx", "ty"),
        P(None, "tx", "ty"),
        P(),
    )
    return jax.shard_map(
        body,
        mesh=mesh,
        in_specs=placed,
        out_specs=(P(None, "tx", "ty"), P(None, "tx", "ty")),
        check_vma=False,
    )
```

```python
import jax
import jax.numpy as jnp
from jax import lax
from jax.experimental import pallas as pl
from jax.experimental.pallas import tpu as pltpu
from jax.sharding import PartitionSpec as P

F32 = jnp.float32
BF16 = jnp.bfloat16

LEV = 4
CX = 64
CY = 128
NSTEP = 10
MIN_STEPS = 5
HALO = 2 * NSTEP
SIDE = 24
EXT = CX + 2 * SIDE
ROWS = LEV * EXT
OWN = 128
TX = 16
TY = 8
CAP = 24
SLOTS = TX * CAP
LISTED = 3 * CAP
PART = 80
GROUP = 16
GROUPS = OWN // GROUP


def iota(shape, dim):
    return lax.broadcasted_iota(jnp.int32, shape, dim)


def pieces(values):
    high = values.astype(BF16)
    return high, (values - high.astype(F32)).astype(BF16)


def pick(onehot, values):
    high, low = pieces(values)
    total = jnp.dot(onehot, high, preferred_element_type=F32)
    return total + jnp.dot(onehot, low, preferred_element_type=F32)


def as_onehot(hit):
    return jnp.where(hit, 1.0, 0.0).astype(BF16)


def slot_tables(tile_ref):
    down = iota((OWN, OWN), 0)
    across = iota((OWN, OWN), 1)
    tile_row = tile_ref[...].astype(F32)
    spread = jnp.broadcast_to(tile_row, (OWN, OWN))
    tile_col = jnp.sum(jnp.where(down == across, spread, 0.0), axis=1, keepdims=True)
    same = spread == tile_col
    rank_row = jnp.sum(jnp.where(same & (down < across), 1.0, 0.0), axis=0, keepdims=True)
    rank_col = jnp.sum(jnp.where(same & (across < down), 1.0, 0.0), axis=1, keepdims=True)
    return tile_row, rank_row, tile_col, rank_col


def write_parts(parts_ref, slots):
    for tile in range(TX):
        for side in (-1, 0, 1):
            source = tile + side
            rows = pl.ds((side + 1) * CAP, CAP)
            if 0 <= source < TX:
                parts_ref[tile, rows, :] = slots[source * CAP : (source + 1) * CAP]
            else:
                parts_ref[tile, rows, :] = jnp.zeros((CAP, 128), F32)


def to_slots(tables, adjoint):
    tile_row, rank_row, _, _ = tables
    slot_row = (tile_row * CAP + rank_row).astype(jnp.int32)
    return pick(as_onehot(iota((SLOTS, OWN), 0) == slot_row), adjoint)


def from_slots(tables, returned):
    _, _, tile_col, rank_col = tables
    slot_col = (tile_col * CAP + rank_col).astype(jnp.int32)
    return pick(as_onehot(iota((OWN, SLOTS), 1) == slot_col), returned)


def listed_columns(tables, column_ref):
    tile_row, _, _, rank_col = tables
    column_row = column_ref[...].astype(F32)
    tile_no = iota((TX, OWN), 0).astype(F32)
    lane = iota((OWN, 128), 1)
    rank = rank_col.astype(jnp.int32)
    total = jnp.zeros((TX, 128), F32)
    for side in (-1, 0, 1):
        mine = jnp.where(tile_row == tile_no + side, column_row, 0.0).astype(BF16)
        place = as_onehot(rank + (side + 1) * CAP == lane)
        total = total + jnp.dot(mine, place, preferred_element_type=F32)
    return total


def live_columns(count_ref, weighted):
    return jnp.where(iota((OWN, OWN), 1) < count_ref[0], weighted.T, 0.0)


def group(number):
    return pl.ds(pl.multiple_of(number * GROUP, GROUP), GROUP)


def load_blocks(operator_ref, blocks_ref, arrived):
    return lambda number: pltpu.make_async_copy(
        operator_ref.at[group(number)], blocks_ref.at[group(number)], arrived.at[number]
    )


def start_all(copy_of):
    for number in range(GROUPS):
        copy_of(number).start()


def first_kernel(
    count_ref, tile_ref, column_ref, innovation_ref, weight_ref, operator_ref,
    parts_ref, adjoint_ref, blocks_ref, arrived,
):
    copy_of = load_blocks(operator_ref, blocks_ref, arrived)
    start_all(copy_of)
    tables = slot_tables(tile_ref)
    listed = listed_columns(tables, column_ref)
    for tile in range(TX):
        parts_ref[tile, pl.ds(LISTED, 8), :] = jnp.broadcast_to(listed[tile : tile + 1], (8, 128))
    down = iota((8, 128), 0)

    def one_group(number, carry):
        here = group(number)
        live = iota((GROUP, OWN), 0) + number * GROUP < count_ref[0]
        weighted = jnp.where(live, weight_ref[here, :] * innovation_ref[here, :], 0.0)
        high = weighted.astype(BF16).astype(F32)
        low = weighted - high
        copy_of(number).wait()
        rows = []
        for k in range(GROUP):
            wide = jnp.broadcast_to(high[k : k + 1], (8, 128))
            narrow = jnp.broadcast_to(low[k : k + 1], (8, 128))
            first = jnp.where(down == 0, wide, 0.0)
            left = jnp.concatenate([jnp.where(down == 1, narrow, first), first], axis=1).astype(BF16)
            right = jnp.concatenate(pieces(blocks_ref[number * GROUP + k]), axis=0)
            product = jnp.dot(left, right, preferred_element_type=F32)
            rows.append(jnp.sum(product, axis=0, keepdims=True))
        adjoint_ref[here, :] = jnp.concatenate(rows, axis=0)
        return carry

    lax.fori_loop(0, GROUPS, one_group, 0)
    write_parts(parts_ref, to_slots(tables, adjoint_ref[...]))


def turn_kernel(operator_ref, turned_ref, blocks_ref, lanes_ref, arrived, left):
    def copy_of(number):
        return pltpu.make_async_copy(
            operator_ref.at[:, group(number), :], blocks_ref.at[number], arrived.at[number]
        )

    def back(number):
        return pltpu.make_async_copy(
            lanes_ref.at[group(number)], turned_ref.at[group(number)], left.at[number]
        )

    start_all(copy_of)

    def one_group(number, carry):
        copy_of(number).wait()
        for k in range(GROUP):
            lanes_ref[number * GROUP + k] = blocks_ref[number, :, k, :].T
        back(number).start()
        return carry

    lax.fori_loop(0, GROUPS, one_group, 0)
    for number in range(GROUPS):
        back(number).wait()


def middle_kernel(
    count_ref, tile_ref, weight_ref, returned_ref, earlier_ref, turned_ref, *refs
):
    *sums_in_ref, parts_ref, adjoint_ref, sums_ref, weight_scr = refs
    tables = slot_tables(tile_ref)
    weight_scr[...] = live_columns(count_ref, weight_ref[...])
    own_segments = from_slots(tables, returned_ref[...])
    segments = own_segments.T

    def one_group(number, total):
        weight = weight_scr[group(number), :]
        for k in range(GROUP):
            block = turned_ref[number * GROUP + k]
            observed = jnp.sum(block * segments, axis=0, keepdims=True)
            total = total + block * (observed * weight[k : k + 1])
        return total

    total = lax.fori_loop(0, GROUPS, one_group, jnp.zeros((OWN, OWN), F32))
    adjoint = total.T
    write_parts(parts_ref, to_slots(tables, adjoint))
    known = jnp.sum(earlier_ref[...] * own_segments, axis=0, keepdims=True)
    new = jnp.sum(adjoint * own_segments, axis=0, keepdims=True)
    before = sums_in_ref[0][2:4] if sums_in_ref else jnp.zeros((2, 128), F32)
    sums = jnp.concatenate([before, known, new, jnp.zeros((4, 128), F32)], axis=0)
    sums_ref[...] = sums
    if sums_in_ref:
        for tile in range(TX):
            parts_ref[tile, pl.ds(LISTED, 8), :] = sums
    adjoint_ref[...] = adjoint + earlier_ref[...]


VMEM_FIRST = 57 << 20
VMEM_TURN = 57 << 20
VMEM_OBSERVE = 16 << 20
SCALARS = pl.BlockSpec(memory_space=pltpu.SMEM)
HERE = pl.BlockSpec(memory_space=pltpu.VMEM)
THERE = pl.BlockSpec(memory_space=pltpu.HBM)
CUBE = (OWN, 128, 128)
PLAIN_PARTS = jax.ShapeDtypeStruct((TX, LISTED, 128), F32)
PARTS = jax.ShapeDtypeStruct((TX, PART, 128), F32)
SQUARE = jax.ShapeDtypeStruct((OWN, 128), F32)
SUMS = jax.ShapeDtypeStruct((8, 128), F32)


def run_first(counts, tile, column, innovation, weight, operator):
    return pl.pallas_call(
        first_kernel,
        in_specs=[SCALARS, HERE, HERE, HERE, HERE, THERE],
        out_specs=[HERE, HERE],
        out_shape=[PARTS, SQUARE],
        scratch_shapes=[
            pltpu.VMEM(CUBE, F32),
            pltpu.SemaphoreType.DMA((GROUPS,)),
        ],
        compiler_params=pltpu.CompilerParams(vmem_limit_bytes=VMEM_FIRST),
        cost_estimate=pl.CostEstimate(flops=4 * 128**3, bytes_accessed=9 << 20, transcendentals=0),
        name="first_adjoint",
    )(counts, tile, column, innovation, weight, operator)


def run_turn(operator):
    return pl.pallas_call(
        turn_kernel,
        in_specs=[THERE],
        out_specs=THERE,
        out_shape=jax.ShapeDtypeStruct(CUBE, F32),
        scratch_shapes=[
            pltpu.VMEM((GROUPS, OWN, GROUP, 128), F32),
            pltpu.VMEM(CUBE, F32),
            pltpu.SemaphoreType.DMA((GROUPS,)),
            pltpu.SemaphoreType.DMA((GROUPS,)),
        ],
        compiler_params=pltpu.CompilerParams(vmem_limit_bytes=VMEM_TURN),
        cost_estimate=pl.CostEstimate(flops=0, bytes_accessed=16 << 20, transcendentals=0),
        name="blocks_on_lanes",
    )(operator)


def run_middle(counts, tile, weight, returned, earlier, turned, *sums):
    return pl.pallas_call(
        middle_kernel,
        in_specs=[SCALARS] + [HERE] * (5 + len(sums)),
        out_specs=[HERE, HERE, HERE],
        out_shape=[PARTS if sums else PLAIN_PARTS, SQUARE, SUMS],
        scratch_shapes=[pltpu.VMEM((OWN, OWN), F32)],
        compiler_params=pltpu.CompilerParams(vmem_limit_bytes=VMEM_OBSERVE),
        cost_estimate=pl.CostEstimate(flops=8 * 128**3, bytes_accessed=10 << 20, transcendentals=0),
        name="observe",
    )(counts, tile, weight, returned, earlier, turned, *sums)


def flat_list(listed, part):
    lane = iota((1, 128), 1)
    words = [jnp.zeros((1, 128), F32)] * (SLOTS // 128)
    for source in range(TX):
        start = CAP * source
        turned = pltpu.roll(listed[source : source + 1], (start - CAP * part) % 128, 1)
        for word in range(start // 128, (start + CAP - 1) // 128 + 1):
            here = (lane + 128 * word >= start) & (lane + 128 * word < start + CAP)
            words[word] = jnp.where(here, turned, words[word])
    return jnp.concatenate(words, axis=1).astype(jnp.int32)


def target_rows(listed):
    west, own, east = (flat_list(listed, part) for part in range(3))
    cell = west & (CX - 1)
    west = jnp.where(cell >= CX - SIDE, (west >> 6) * SIDE + cell - (CX - SIDE), -1)
    cell = east & (CX - 1)
    east = jnp.where(cell < SIDE, (east >> 6) * SIDE + cell, -1)
    return jnp.concatenate([west, own, east, jnp.zeros((5, SLOTS), jnp.int32)], axis=0)


def scatter(field_ref, parts_ref, rows_ref, sigma_ext_ref):
    at = 0
    for part, width in ((0, SIDE), (1, CX), (2, SIDE)):
        values = jnp.concatenate(
            [parts_ref[source, pl.ds(part * CAP, CAP), :] for source in range(TX)], axis=0
        )
        onehot = as_onehot(iota((LEV * width, SLOTS), 0) == rows_ref[part : part + 1, :])
        total = jnp.dot(
            jnp.concatenate([onehot, onehot], axis=1),
            jnp.concatenate(pieces(values), axis=0),
            preferred_element_type=F32,
        )
        for level in range(LEV):
            here = pl.ds(level * EXT + at, width)
            field_ref[here, :] = total[level * width : (level + 1) * width] * sigma_ext_ref[here, :]
        at += width


def edges(field, even):
    lane = iota((EXT, 128), 1)
    west = jnp.zeros((EXT, 128), F32)
    east = jnp.zeros((EXT, 128), F32)
    for level in range(LEV):
        part = field[level * EXT : (level + 1) * EXT]
        here = (lane >= 32 * level) & (lane < 32 * level + HALO)
        low = pltpu.roll(part, 32 * level, 1) if level else part
        west = jnp.where(here, low, west)
        east = jnp.where(here, pltpu.roll(part, (32 * level + HALO) % 128, 1), east)
    return jnp.where(even, east, west), jnp.where(even, west, east)


def parity(axis):
    return lax.axis_index(axis) % 2 == 0


def prepare_kernel(mask_ref, diffusivity_ref, sigma_ref, kappa_ref, pair_ref, other_ref):
    even = parity("tx")
    for level in range(LEV):
        kappa = diffusivity_ref[level] * mask_ref[level].astype(F32)
        kappa_ref[level] = kappa
        for number, values in ((0, kappa), (1, sigma_ref[level])):
            low, high = values[:SIDE], values[CX - SIDE :]
            pair_ref[number, level] = jnp.where(even, high, low)
            other_ref[number, level] = jnp.where(even, low, high)


def open_kernel(
    parts_ref, sigma_ref, kappa_ref, near_ref, far_ref,
    field_ref, sigma_ext_ref, kappa_ext_ref, pair_ref, other_ref, listed_ref, rows_ref,
):
    row_no = lax.axis_index("tx")
    even_row = parity("tx")
    even = parity("ty")
    not_first = jnp.where(row_no > 0, 1.0, 0.0)
    not_last = jnp.where(row_no < TX - 1, 1.0, 0.0)
    for level in range(LEV):
        base = level * EXT
        near_k, far_k = near_ref[0, level], far_ref[0, level]
        near_s, far_s = near_ref[1, level], far_ref[1, level]
        kappa_ext_ref[pl.ds(base, SIDE), :] = jnp.where(even_row, far_k, near_k) * not_first
        kappa_ext_ref[pl.ds(base + SIDE, CX), :] = kappa_ref[level]
        kappa_ext_ref[pl.ds(base + SIDE + CX, SIDE), :] = jnp.where(even_row, near_k, far_k) * not_last
        sigma_ext_ref[pl.ds(base, SIDE), :] = jnp.where(even_row, far_s, near_s)
        sigma_ext_ref[pl.ds(base + SIDE, CX), :] = sigma_ref[level]
        sigma_ext_ref[pl.ds(base + SIDE + CX, SIDE), :] = jnp.where(even_row, near_s, far_s)
    sigma_ext_ref[...] = jnp.where(kappa_ext_ref[...] > 0.0, sigma_ext_ref[...], 0.0)
    listed = jnp.concatenate([parts_ref[k, pl.ds(LISTED, 1), :] for k in range(TX)], axis=0)
    listed_ref[...] = listed
    rows_ref[...] = target_rows(listed)
    scatter(field_ref, parts_ref, rows_ref, sigma_ext_ref)
    pair_ref[0], other_ref[0] = edges(field_ref[...], even)
    pair_ref[1], other_ref[1] = edges(kappa_ext_ref[...], even)


def bring_kernel(listed_ref, _, brought_ref):
    brought_ref[...] = listed_ref[:8]


def gather_kernel(parts_ref, sigma_ext_ref, rows_ref, field_ref, pair_ref, other_ref):
    scatter(field_ref, parts_ref, rows_ref, sigma_ext_ref)
    pair_ref[0], other_ref[0] = edges(field_ref[...], parity("ty"))


def last_gather_kernel(parts_ref, sigma_ext_ref, rows_ref, field_ref, pair_ref, other_ref, sums_ref):
    scatter(field_ref, parts_ref, rows_ref, sigma_ext_ref)
    pair_ref[0, pl.ds(0, EXT), :], other_ref[0, pl.ds(0, EXT), :] = edges(field_ref[...], parity("ty"))
    sums = parts_ref[0, pl.ds(LISTED, 8), :]
    for source in range(1, TX):
        sums = sums + parts_ref[source, pl.ds(LISTED, 8), :]
    pair_ref[0, pl.ds(EXT, 8), :] = sums
    other_ref[0, pl.ds(EXT, 8), :] = sums
    sums_ref[...] = sums


def meet_kernel(sums_ref, near_ref, pair_ref):
    pair_ref[...] = sums_ref[...] + near_ref[0, pl.ds(EXT, 8), :]


def widen(work_ref, field_ref, west_of, east_of):
    lane = iota((EXT, 128), 1)
    for level in range(LEV):
        part = field_ref[pl.ds(level * EXT, EXT), :]
        first = jnp.where(
            lane < HALO, west_of(level), pltpu.roll(part, HALO, 1)
        )
        second = jnp.where(
            lane >= 128 - HALO,
            east_of(level),
            pltpu.roll(part, 128 - HALO, 1),
        )
        work_ref[pl.ds(level, EXT, stride=8), :] = first
        work_ref[pl.ds(LEV + level, EXT, stride=8), :] = second


def tile_part(work_ref, level):
    lane = iota((CX, 128), 1)
    first = work_ref[pl.ds(SIDE * 8 + level, CX, stride=8), :]
    second = work_ref[pl.ds(SIDE * 8 + LEV + level, CX, stride=8), :]
    return jnp.where(lane < CY // 2, pltpu.roll(first, 128 - HALO, 1), pltpu.roll(second, HALO, 1))


def level_counts(count_ref):
    level = iota((8, 128), 0) % LEV
    counts = jnp.full((8, 128), count_ref[0], jnp.int32)
    for k in range(1, LEV):
        counts = jnp.where(level == k, count_ref[k], counts)
    return counts


def sweeps(work_ref, along_ref, across_ref, counts, first_row, end_row):
    def one(number, masked, first_row, end_row):
        active = counts > number
        flux = None
        now = work_ref[pl.ds(first_row * 8, 8), :]
        for row in range(first_row, end_row):
            here = pl.ds(row * 8, 8)
            side = across_ref[here, :] * (pltpu.roll(now, 127, 1) - now)
            change = side - pltpu.roll(side, 1, 1)
            if flux is not None:
                change = change - flux
            after = None
            if row + 1 < end_row:
                after = work_ref[pl.ds((row + 1) * 8, 8), :]
                flux = along_ref[here, :] * (after - now)
                change = change + flux
            if masked:
                change = jnp.where(active, change, 0.0)
            work_ref[here, :] = now + change
            now = after

    for number in range(NSTEP):
        one(number, number >= MIN_STEPS, first_row + number, end_row - number)


def faces(work_ref, along_ref, across_ref):
    def mask_of(kappa):
        return jnp.where(kappa > 0.0, 1.0, 0.0)

    for row in range(EXT):
        here = pl.ds(row * 8, 8)
        kappa = work_ref[here, :]
        mask = mask_of(kappa)
        if row + 1 < EXT:
            after = work_ref[pl.ds((row + 1) * 8, 8), :]
            along_ref[here, :] = 0.5 * (mask * after + kappa * mask_of(after))
        else:
            along_ref[here, :] = jnp.zeros((8, 128), F32)
        beside = pltpu.roll(kappa, 127, 1)
        across_ref[here, :] = 0.5 * (mask * beside + kappa * mask_of(beside))


def strips(packed):
    west, east = packed

    def west_of(level):
        return pltpu.roll(west, 128 - 32 * level, 1) if level else west

    def east_of(level):
        return pltpu.roll(east, (2 * 128 - HALO - 32 * level) % 128, 1)

    return west_of, east_of


def from_pairs(near_ref, far_ref, which):
    near, far = near_ref[which, pl.ds(0, EXT), :], far_ref[which, pl.ds(0, EXT), :]
    even = parity("ty")
    return jnp.where(even, far, near), jnp.where(even, near, far)


def send_segments(picked_ref, listed_ref, segments):
    listed = jnp.concatenate([listed_ref[...], jnp.zeros((128 - TX, 128), F32)], axis=0).T
    mine = listed[CAP : 2 * CAP].astype(jnp.int32)
    lane = iota((CAP, LEV * CX), 1)
    hits = [
        jnp.where(mine[:, source : source + 1] == lane, 1.0, 0.0) for source in range(TX)
    ]
    onehot = jnp.concatenate(hits, axis=0).astype(BF16)
    picked_ref[...] = pick(onehot, segments)


INNER = (SIDE - NSTEP, SIDE + CX + NSTEP)
OUTER = (SIDE - HALO, SIDE + CX + HALO)


def spread_first_kernel(
    count_ref, field_ref, kappa_ext_ref, near_ref, far_ref, sigma_ref, listed_ref, _,
    picked_ref, once_ref, twice_ref, along_ref, across_ref, work_ref,
):
    band = lax.axis_index("ty")
    west, east = from_pairs(near_ref, far_ref, 1)
    west = west * jnp.where(band > 0, 1.0, 0.0)
    east = east * jnp.where(band < TY - 1, 1.0, 0.0)
    widen(work_ref, kappa_ext_ref, *strips((west, east)))
    faces(work_ref, along_ref, across_ref)
    widen(work_ref, field_ref, *strips(from_pairs(near_ref, far_ref, 0)))
    counts = level_counts(count_ref)
    sweeps(work_ref, along_ref, across_ref, counts, *OUTER)
    for level in range(LEV):
        once_ref[level] = tile_part(work_ref, level)
    sweeps(work_ref, along_ref, across_ref, counts, *INNER)
    parts = []
    for level in range(LEV):
        part = tile_part(work_ref, level)
        twice_ref[level] = part
        parts.append(part * sigma_ref[level])
    send_segments(picked_ref, listed_ref, jnp.concatenate(parts, axis=0))


def spread_next_kernel(
    count_ref, field_ref, near_ref, far_ref, sigma_ref, listed_ref, along_ref, across_ref,
    once_ref, twice_ref,
    picked_ref, image_ref, work_ref,
):
    widen(work_ref, field_ref, *strips(from_pairs(near_ref, far_ref, 0)))
    counts = level_counts(count_ref)
    sweeps(work_ref, along_ref, across_ref, counts, *OUTER)
    for level in range(LEV):
        image_ref[level] = once_ref[level] + tile_part(work_ref, level)
    sweeps(work_ref, along_ref, across_ref, counts, *INNER)
    parts = []
    for level in range(LEV):
        parts.append((twice_ref[level] + tile_part(work_ref, level)) * sigma_ref[level])
    send_segments(picked_ref, listed_ref, jnp.concatenate(parts, axis=0))


def spread_last_kernel(count_ref, field_ref, near_ref, far_ref, along_ref, across_ref, last_ref, work_ref):
    widen(work_ref, field_ref, *strips(from_pairs(near_ref, far_ref, 0)))
    sweeps(work_ref, along_ref, across_ref, level_counts(count_ref), *INNER)
    for level in range(LEV):
        last_ref[level] = tile_part(work_ref, level)


def finish_kernel(
    last_ref, here_ref, one_ref, two_ref, three_ref, start_ref, image_ref, control_ref, residual_ref
):
    sums = (here_ref[...] + one_ref[...]) + (two_ref[...] + three_ref[...])
    sums = jnp.sum(sums, axis=1, keepdims=True)
    start_start = sums[0:1]
    start_image = sums[0:1] + sums[1:2]
    image_image = sums[2:3]
    image_second = sums[2:3] + sums[3:4]
    step = start_start / start_image
    norm = step * step * image_image - 2.0 * step * start_image + start_start
    ratio = norm / start_start
    next_next = start_image - 2.0 * step * image_image + step * step * image_second
    next_start = start_image - step * image_image
    curvature = next_next + 2.0 * ratio * next_start + ratio * ratio * start_image
    second = norm / curvature
    for level in range(LEV):
        start = start_ref[level]
        image = image_ref[level]
        twice = image + last_ref[level]
        remainder = start - step * image
        direction = remainder + ratio * start
        curved = (1.0 + ratio) * image - step * twice
        control_ref[level] = step * start + second * direction
        residual_ref[level] = remainder - second * curved


WORK = [pltpu.VMEM((EXT * 8, 128), F32)]
TILE = jax.ShapeDtypeStruct((LEV, CX, CY), F32)
WIDENED = jax.ShapeDtypeStruct((ROWS, 128), F32)
LAID = jax.ShapeDtypeStruct((EXT * 8, 128), F32)
TARGETS = jax.ShapeDtypeStruct((8, SLOTS), jnp.int32)
LISTS = jax.ShapeDtypeStruct((TX, 128), F32)
PICKED = jax.ShapeDtypeStruct((SLOTS, 128), F32)


def edge_shape(number, more=0):
    return jax.ShapeDtypeStruct((number, EXT + more, 128), F32)


def tile_call(kernel, out_shape, scalars, arrays, name, scratch=(), after=()):
    return pl.pallas_call(
        kernel,
        in_specs=[SCALARS] * len(scalars) + [HERE] * len(arrays) + [HERE] * len(after),
        out_specs=[HERE] * len(out_shape),
        out_shape=list(out_shape),
        scratch_shapes=list(scratch),
        compiler_params=pltpu.CompilerParams(vmem_limit_bytes=16 << 20),
        name=name,
    )(*scalars, *arrays, *after)


def swap_neighbours(for_pair, for_other, axis):
    count = lax.axis_size(axis)
    pairs = [(i, i ^ 1) for i in range(count)]
    others = [(i, (i + (1 if i % 2 else -1)) % count) for i in range(count)]
    return lax.ppermute(for_pair, axis, pairs), lax.ppermute(for_other, axis, others)


def exchange(parts):
    return lax.all_to_all(parts, "tx", split_axis=0, concat_axis=0, tiled=True)


def body(
    innovation,
    obs_weight,
    obs_operator,
    block_tile,
    owner_counts,
    block_column,
    sea_mask,
    diffusivity,
    background_std,
    step_counts,
):
    tile = block_tile.reshape(1, OWN)
    column = block_column.reshape(1, OWN)

    rows_shape = jax.ShapeDtypeStruct((2, LEV, SIDE, 128), F32)
    kappa, pair, other = tile_call(
        prepare_kernel,
        (TILE, rows_shape, rows_shape),
        (),
        (sea_mask, diffusivity, background_std),
        "prepare",
    )
    near_x, far_x = swap_neighbours(pair, other, "tx")
    parts, adjoint = run_first(owner_counts, tile, column, innovation, obs_weight, obs_operator)
    turned = run_turn(obs_operator)
    parts, turned = lax.optimization_barrier((exchange(parts), turned))
    field, sigma_ext, kappa_ext, pair, other, listed, rows = tile_call(
        open_kernel,
        (WIDENED, WIDENED, WIDENED, edge_shape(2), edge_shape(2), LISTS, TARGETS),
        (),
        (parts, background_std, kappa, near_x, far_x),
        "open_tile",
    )
    near, far = swap_neighbours(pair, other, "ty")
    brought = tile_call(bring_kernel, (SUMS,), (), (listed, turned), "bring_blocks")
    picked, once, twice, along, across = tile_call(
        spread_first_kernel,
        (PICKED, TILE, TILE, LAID, LAID),
        (step_counts,),
        (field, kappa_ext, near, far, background_std, listed),
        "spread_first",
        WORK,
        after=brought,
    )
    returned = exchange(picked.reshape(TX, CAP, 128)).reshape(SLOTS, 128)
    parts, adjoint, sums = run_middle(owner_counts, tile, obs_weight, returned, adjoint, turned)
    parts = exchange(parts)
    field, pair, other = tile_call(
        gather_kernel,
        (WIDENED, edge_shape(1), edge_shape(1)),
        (),
        (parts, sigma_ext, rows),
        "gather_tile",
    )
    near, far = swap_neighbours(pair, other, "ty")
    picked, image = tile_call(
        spread_next_kernel,
        (PICKED, TILE),
        (step_counts,),
        (field, near, far, background_std, listed, along, across, once, twice),
        "spread_next",
        WORK,
    )
    returned = exchange(picked.reshape(TX, CAP, 128)).reshape(SLOTS, 128)
    parts, adjoint, sums = run_middle(
        owner_counts, tile, obs_weight, returned, adjoint, turned, sums
    )
    parts = exchange(parts)
    field, pair, other, sums = tile_call(
        last_gather_kernel,
        (WIDENED, edge_shape(1, 8), edge_shape(1, 8), SUMS),
        (),
        (parts, sigma_ext, rows),
        "gather_last",
    )
    near, far = swap_neighbours(pair, other, "ty")
    chip = tile_call(meet_kernel, (SUMS,), (), (sums, near), "meet")[0]
    chips = [
        lax.ppermute(chip, "ty", [(i, i ^ k) for i in range(lax.axis_size("ty"))]) for k in (2, 4, 6)
    ]
    last = tile_call(
        spread_last_kernel,
        (TILE,),
        (step_counts,),
        (field, near, far, along, across),
        "spread_last",
        WORK,
    )[0]
    control_field, residual = tile_call(
        finish_kernel, (TILE, TILE), (), (last, chip, *chips, once, image), "finish"
    )
    return control_field, residual


def solution(mesh):
    placed = (
        P(("tx", "ty"), None),
        P(("tx", "ty"), None),
        P(("tx", "ty"), None, None),
        P(("tx", "ty"), None),
        P(("tx", "ty")),
        P(("tx", "ty")),
        P(None, "tx", "ty"),
        P(None, "tx", "ty"),
        P(None, "tx", "ty"),
        P(),
    )
    return jax.shard_map(
        body,
        mesh=mesh,
        in_specs=placed,
        out_specs=(P(None, "tx", "ty"), P(None, "tx", "ty")),
        check_vma=False,
    )
```

```python
import jax
import jax.numpy as jnp
from jax import lax
from jax.experimental import pallas as pl
from jax.experimental.pallas import tpu as pltpu
from jax.sharding import PartitionSpec as P

F32 = jnp.float32
BF16 = jnp.bfloat16

LEV = 4
CX = 64
CY = 128
NSTEP = 10
MIN_STEPS = 5
HALO = 2 * NSTEP
SIDE = 24
EXT = CX + 2 * SIDE
ROWS = LEV * EXT
OWN = 128
TX = 16
TY = 8
CAP = 24
SLOTS = TX * CAP
LISTED = 3 * CAP
PART = 80
GROUP = 16
GROUPS = OWN // GROUP


def iota(shape, dim):
    return lax.broadcasted_iota(jnp.int32, shape, dim)


def pieces(values):
    high = values.astype(BF16)
    return high, (values - high.astype(F32)).astype(BF16)


def pick(onehot, values):
    high, low = pieces(values)
    total = jnp.dot(onehot, high, preferred_element_type=F32)
    return total + jnp.dot(onehot, low, preferred_element_type=F32)


def as_onehot(hit):
    return jnp.where(hit, 1.0, 0.0).astype(BF16)


def slot_tables(tile_ref):
    down = iota((OWN, OWN), 0)
    across = iota((OWN, OWN), 1)
    tile_row = tile_ref[...].astype(F32)
    spread = jnp.broadcast_to(tile_row, (OWN, OWN))
    tile_col = jnp.sum(jnp.where(down == across, spread, 0.0), axis=1, keepdims=True)
    same = spread == tile_col
    rank_row = jnp.sum(jnp.where(same & (down < across), 1.0, 0.0), axis=0, keepdims=True)
    rank_col = jnp.sum(jnp.where(same & (across < down), 1.0, 0.0), axis=1, keepdims=True)
    return tile_row, rank_row, tile_col, rank_col


def write_parts(parts_ref, slots):
    for tile in range(TX):
        for side in (-1, 0, 1):
            source = tile + side
            rows = pl.ds((side + 1) * CAP, CAP)
            if 0 <= source < TX:
                parts_ref[tile, rows, :] = slots[source * CAP : (source + 1) * CAP]
            else:
                parts_ref[tile, rows, :] = jnp.zeros((CAP, 128), F32)


def to_slots(tables, adjoint):
    tile_row, rank_row, _, _ = tables
    slot_row = (tile_row * CAP + rank_row).astype(jnp.int32)
    return pick(as_onehot(iota((SLOTS, OWN), 0) == slot_row), adjoint)


def from_slots(tables, returned):
    _, _, tile_col, rank_col = tables
    slot_col = (tile_col * CAP + rank_col).astype(jnp.int32)
    return pick(as_onehot(iota((OWN, SLOTS), 1) == slot_col), returned)


def listed_columns(tables, column_ref):
    tile_row, _, _, rank_col = tables
    column_row = column_ref[...].astype(F32)
    tile_no = iota((TX, OWN), 0).astype(F32)
    lane = iota((OWN, 128), 1)
    rank = rank_col.astype(jnp.int32)
    total = jnp.zeros((TX, 128), F32)
    for side in (-1, 0, 1):
        mine = jnp.where(tile_row == tile_no + side, column_row, 0.0).astype(BF16)
        place = as_onehot(rank + (side + 1) * CAP == lane)
        total = total + jnp.dot(mine, place, preferred_element_type=F32)
    return total


def live_columns(count_ref, weighted):
    return jnp.where(iota((OWN, OWN), 1) < count_ref[0], weighted.T, 0.0)


def group(number):
    return pl.ds(pl.multiple_of(number * GROUP, GROUP), GROUP)


def load_blocks(operator_ref, blocks_ref, arrived):
    return lambda number: pltpu.make_async_copy(
        operator_ref.at[group(number)], blocks_ref.at[group(number)], arrived.at[number]
    )


def start_all(copy_of):
    for number in range(GROUPS):
        copy_of(number).start()


def first_kernel(
    count_ref, tile_ref, column_ref, innovation_ref, weight_ref, operator_ref,
    parts_ref, adjoint_ref, blocks_ref, arrived,
):
    copy_of = load_blocks(operator_ref, blocks_ref, arrived)
    start_all(copy_of)
    tables = slot_tables(tile_ref)
    listed = listed_columns(tables, column_ref)
    for tile in range(TX):
        parts_ref[tile, pl.ds(LISTED, 8), :] = jnp.broadcast_to(listed[tile : tile + 1], (8, 128))
    down = iota((8, 128), 0)

    def one_group(number, carry):
        here = group(number)
        live = iota((GROUP, OWN), 0) + number * GROUP < count_ref[0]
        weighted = jnp.where(live, weight_ref[here, :] * innovation_ref[here, :], 0.0)
        high = weighted.astype(BF16).astype(F32)
        low = weighted - high
        copy_of(number).wait()
        rows = []
        for k in range(GROUP):
            wide = jnp.broadcast_to(high[k : k + 1], (8, 128))
            narrow = jnp.broadcast_to(low[k : k + 1], (8, 128))
            first = jnp.where(down == 0, wide, 0.0)
            left = jnp.concatenate([jnp.where(down == 1, narrow, first), first], axis=1).astype(BF16)
            right = jnp.concatenate(pieces(blocks_ref[number * GROUP + k]), axis=0)
            product = jnp.dot(left, right, preferred_element_type=F32)
            rows.append(jnp.sum(product, axis=0, keepdims=True))
        adjoint_ref[here, :] = jnp.concatenate(rows, axis=0)
        return carry

    lax.fori_loop(0, GROUPS, one_group, 0)
    write_parts(parts_ref, to_slots(tables, adjoint_ref[...]))


def turn_kernel(operator_ref, turned_ref, blocks_ref, lanes_ref, arrived, left):
    def copy_of(number):
        return pltpu.make_async_copy(
            operator_ref.at[:, group(number), :], blocks_ref.at[number], arrived.at[number]
        )

    def back(number):
        return pltpu.make_async_copy(
            lanes_ref.at[group(number)], turned_ref.at[group(number)], left.at[number]
        )

    start_all(copy_of)

    def one_group(number, carry):
        copy_of(number).wait()
        for k in range(GROUP):
            lanes_ref[number * GROUP + k] = blocks_ref[number, :, k, :].T
        back(number).start()
        return carry

    lax.fori_loop(0, GROUPS, one_group, 0)
    for number in range(GROUPS):
        back(number).wait()


def middle_kernel(
    count_ref, tile_ref, weight_ref, returned_ref, earlier_ref, turned_ref, *refs
):
    *sums_in_ref, parts_ref, adjoint_ref, sums_ref, weight_scr = refs
    tables = slot_tables(tile_ref)
    weight_scr[...] = live_columns(count_ref, weight_ref[...])
    own_segments = from_slots(tables, returned_ref[...])
    segments = own_segments.T

    def one_group(number, total):
        weight = weight_scr[group(number), :]
        for k in range(GROUP):
            block = turned_ref[number * GROUP + k]
            observed = jnp.sum(block * segments, axis=0, keepdims=True)
            total = total + block * (observed * weight[k : k + 1])
        return total

    total = lax.fori_loop(0, GROUPS, one_group, jnp.zeros((OWN, OWN), F32))
    adjoint = total.T
    write_parts(parts_ref, to_slots(tables, adjoint))
    known = jnp.sum(earlier_ref[...] * own_segments, axis=0, keepdims=True)
    new = jnp.sum(adjoint * own_segments, axis=0, keepdims=True)
    before = sums_in_ref[0][2:4] if sums_in_ref else jnp.zeros((2, 128), F32)
    sums = jnp.concatenate([before, known, new, jnp.zeros((4, 128), F32)], axis=0)
    sums_ref[...] = sums
    if sums_in_ref:
        for tile in range(TX):
            parts_ref[tile, pl.ds(LISTED, 8), :] = sums
    adjoint_ref[...] = adjoint + earlier_ref[...]


VMEM_FIRST = 57 << 20
VMEM_TURN = 57 << 20
VMEM_OBSERVE = 16 << 20
SCALARS = pl.BlockSpec(memory_space=pltpu.SMEM)
HERE = pl.BlockSpec(memory_space=pltpu.VMEM)
THERE = pl.BlockSpec(memory_space=pltpu.HBM)
CUBE = (OWN, 128, 128)
PLAIN_PARTS = jax.ShapeDtypeStruct((TX, LISTED, 128), F32)
PARTS = jax.ShapeDtypeStruct((TX, PART, 128), F32)
SQUARE = jax.ShapeDtypeStruct((OWN, 128), F32)
SUMS = jax.ShapeDtypeStruct((8, 128), F32)


def run_first(counts, tile, column, innovation, weight, operator):
    return pl.pallas_call(
        first_kernel,
        in_specs=[SCALARS, HERE, HERE, HERE, HERE, THERE],
        out_specs=[HERE, HERE],
        out_shape=[PARTS, SQUARE],
        scratch_shapes=[
            pltpu.VMEM(CUBE, F32),
            pltpu.SemaphoreType.DMA((GROUPS,)),
        ],
        compiler_params=pltpu.CompilerParams(vmem_limit_bytes=VMEM_FIRST),
        cost_estimate=pl.CostEstimate(flops=4 * 128**3, bytes_accessed=9 << 20, transcendentals=0),
        name="first_adjoint",
    )(counts, tile, column, innovation, weight, operator)


def run_turn(operator):
    return pl.pallas_call(
        turn_kernel,
        in_specs=[THERE],
        out_specs=THERE,
        out_shape=jax.ShapeDtypeStruct(CUBE, F32),
        scratch_shapes=[
            pltpu.VMEM((GROUPS + 1, OWN, GROUP, 128), F32),
            pltpu.VMEM(CUBE, F32),
            pltpu.SemaphoreType.DMA((GROUPS,)),
            pltpu.SemaphoreType.DMA((GROUPS,)),
        ],
        compiler_params=pltpu.CompilerParams(vmem_limit_bytes=VMEM_TURN),
        cost_estimate=pl.CostEstimate(flops=0, bytes_accessed=16 << 20, transcendentals=0),
        name="blocks_on_lanes",
    )(operator)


def run_middle(counts, tile, weight, returned, earlier, turned, *sums):
    return pl.pallas_call(
        middle_kernel,
        in_specs=[SCALARS] + [HERE] * (5 + len(sums)),
        out_specs=[HERE, HERE, HERE],
        out_shape=[PARTS if sums else PLAIN_PARTS, SQUARE, SUMS],
        scratch_shapes=[pltpu.VMEM((OWN, OWN), F32)],
        compiler_params=pltpu.CompilerParams(vmem_limit_bytes=VMEM_OBSERVE),
        cost_estimate=pl.CostEstimate(flops=8 * 128**3, bytes_accessed=10 << 20, transcendentals=0),
        name="observe",
    )(counts, tile, weight, returned, earlier, turned, *sums)


def flat_list(listed, part):
    lane = iota((1, 128), 1)
    words = [jnp.zeros((1, 128), F32)] * (SLOTS // 128)
    for source in range(TX):
        start = CAP * source
        turned = pltpu.roll(listed[source : source + 1], (start - CAP * part) % 128, 1)
        for word in range(start // 128, (start + CAP - 1) // 128 + 1):
            here = (lane + 128 * word >= start) & (lane + 128 * word < start + CAP)
            words[word] = jnp.where(here, turned, words[word])
    return jnp.concatenate(words, axis=1).astype(jnp.int32)


def target_rows(listed):
    west, own, east = (flat_list(listed, part) for part in range(3))
    cell = west & (CX - 1)
    west = jnp.where(cell >= CX - SIDE, (west >> 6) * SIDE + cell - (CX - SIDE), -1)
    cell = east & (CX - 1)
    east = jnp.where(cell < SIDE, (east >> 6) * SIDE + cell, -1)
    return jnp.concatenate([west, own, east, jnp.zeros((5, SLOTS), jnp.int32)], axis=0)


def scatter(field_ref, parts_ref, rows_ref, sigma_ext_ref):
    at = 0
    for part, width in ((0, SIDE), (1, CX), (2, SIDE)):
        values = jnp.concatenate(
            [parts_ref[source, pl.ds(part * CAP, CAP), :] for source in range(TX)], axis=0
        )
        onehot = as_onehot(iota((LEV * width, SLOTS), 0) == rows_ref[part : part + 1, :])
        total = jnp.dot(
            jnp.concatenate([onehot, onehot], axis=1),
            jnp.concatenate(pieces(values), axis=0),
            preferred_element_type=F32,
        )
        for level in range(LEV):
            here = pl.ds(level * EXT + at, width)
            field_ref[here, :] = total[level * width : (level + 1) * width] * sigma_ext_ref[here, :]
        at += width


def edges(field, even):
    lane = iota((EXT, 128), 1)
    west = jnp.zeros((EXT, 128), F32)
    east = jnp.zeros((EXT, 128), F32)
    for level in range(LEV):
        part = field[level * EXT : (level + 1) * EXT]
        here = (lane >= 32 * level) & (lane < 32 * level + HALO)
        low = pltpu.roll(part, 32 * level, 1) if level else part
        west = jnp.where(here, low, west)
        east = jnp.where(here, pltpu.roll(part, (32 * level + HALO) % 128, 1), east)
    return jnp.where(even, east, west), jnp.where(even, west, east)


def parity(axis):
    return lax.axis_index(axis) % 2 == 0


def prepare_kernel(mask_ref, diffusivity_ref, sigma_ref, kappa_ref, pair_ref, other_ref):
    even = parity("tx")
    for level in range(LEV):
        kappa = diffusivity_ref[level] * mask_ref[level].astype(F32)
        kappa_ref[level] = kappa
        for number, values in ((0, kappa), (1, sigma_ref[level])):
            low, high = values[:SIDE], values[CX - SIDE :]
            pair_ref[number, level] = jnp.where(even, high, low)
            other_ref[number, level] = jnp.where(even, low, high)


def open_kernel(
    parts_ref, sigma_ref, kappa_ref, near_ref, far_ref,
    field_ref, sigma_ext_ref, kappa_ext_ref, pair_ref, other_ref, listed_ref, rows_ref,
):
    row_no = lax.axis_index("tx")
    even_row = parity("tx")
    even = parity("ty")
    not_first = jnp.where(row_no > 0, 1.0, 0.0)
    not_last = jnp.where(row_no < TX - 1, 1.0, 0.0)
    for level in range(LEV):
        base = level * EXT
        near_k, far_k = near_ref[0, level], far_ref[0, level]
        near_s, far_s = near_ref[1, level], far_ref[1, level]
        kappa_ext_ref[pl.ds(base, SIDE), :] = jnp.where(even_row, far_k, near_k) * not_first
        kappa_ext_ref[pl.ds(base + SIDE, CX), :] = kappa_ref[level]
        kappa_ext_ref[pl.ds(base + SIDE + CX, SIDE), :] = jnp.where(even_row, near_k, far_k) * not_last
        sigma_ext_ref[pl.ds(base, SIDE), :] = jnp.where(even_row, far_s, near_s)
        sigma_ext_ref[pl.ds(base + SIDE, CX), :] = sigma_ref[level]
        sigma_ext_ref[pl.ds(base + SIDE + CX, SIDE), :] = jnp.where(even_row, near_s, far_s)
    sigma_ext_ref[...] = jnp.where(kappa_ext_ref[...] > 0.0, sigma_ext_ref[...], 0.0)
    listed = jnp.concatenate([parts_ref[k, pl.ds(LISTED, 1), :] for k in range(TX)], axis=0)
    listed_ref[...] = listed
    rows_ref[...] = target_rows(listed)
    scatter(field_ref, parts_ref, rows_ref, sigma_ext_ref)
    pair_ref[0], other_ref[0] = edges(field_ref[...], even)
    pair_ref[1], other_ref[1] = edges(kappa_ext_ref[...], even)


def bring_kernel(listed_ref, _, brought_ref):
    brought_ref[...] = listed_ref[:8]


def gather_kernel(parts_ref, sigma_ext_ref, rows_ref, field_ref, pair_ref, other_ref):
    scatter(field_ref, parts_ref, rows_ref, sigma_ext_ref)
    pair_ref[0], other_ref[0] = edges(field_ref[...], parity("ty"))


def last_gather_kernel(parts_ref, sigma_ext_ref, rows_ref, field_ref, pair_ref, other_ref, sums_ref):
    scatter(field_ref, parts_ref, rows_ref, sigma_ext_ref)
    pair_ref[0, pl.ds(0, EXT), :], other_ref[0, pl.ds(0, EXT), :] = edges(field_ref[...], parity("ty"))
    sums = parts_ref[0, pl.ds(LISTED, 8), :]
    for source in range(1, TX):
        sums = sums + parts_ref[source, pl.ds(LISTED, 8), :]
    pair_ref[0, pl.ds(EXT, 8), :] = sums
    other_ref[0, pl.ds(EXT, 8), :] = sums
    sums_ref[...] = sums


def meet_kernel(sums_ref, near_ref, pair_ref):
    pair_ref[...] = sums_ref[...] + near_ref[0, pl.ds(EXT, 8), :]


def widen(work_ref, field_ref, west_of, east_of):
    lane = iota((EXT, 128), 1)
    for level in range(LEV):
        part = field_ref[pl.ds(level * EXT, EXT), :]
        first = jnp.where(
            lane < HALO, west_of(level), pltpu.roll(part, HALO, 1)
        )
        second = jnp.where(
            lane >= 128 - HALO,
            east_of(level),
            pltpu.roll(part, 128 - HALO, 1),
        )
        work_ref[pl.ds(level, EXT, stride=8), :] = first
        work_ref[pl.ds(LEV + level, EXT, stride=8), :] = second


def tile_part(work_ref, level):
    lane = iota((CX, 128), 1)
    first = work_ref[pl.ds(SIDE * 8 + level, CX, stride=8), :]
    second = work_ref[pl.ds(SIDE * 8 + LEV + level, CX, stride=8), :]
    return jnp.where(lane < CY // 2, pltpu.roll(first, 128 - HALO, 1), pltpu.roll(second, HALO, 1))


def level_counts(count_ref):
    level = iota((8, 128), 0) % LEV
    counts = jnp.full((8, 128), count_ref[0], jnp.int32)
    for k in range(1, LEV):
        counts = jnp.where(level == k, count_ref[k], counts)
    return counts


def sweeps(work_ref, along_ref, across_ref, counts, first_row, end_row):
    def one(number, masked, first_row, end_row):
        active = counts > number
        flux = None
        now = work_ref[pl.ds(first_row * 8, 8), :]
        for row in range(first_row, end_row):
            here = pl.ds(row * 8, 8)
            side = across_ref[here, :] * (pltpu.roll(now, 127, 1) - now)
            change = side - pltpu.roll(side, 1, 1)
            if flux is not None:
                change = change - flux
            after = None
            if row + 1 < end_row:
                after = work_ref[pl.ds((row + 1) * 8, 8), :]
                flux = along_ref[here, :] * (after - now)
                change = change + flux
            if masked:
                change = jnp.where(active, change, 0.0)
            work_ref[here, :] = now + change
            now = after

    for number in range(NSTEP):
        one(number, number >= MIN_STEPS, first_row + number, end_row - number)


def faces(work_ref, along_ref, across_ref):
    def mask_of(kappa):
        return jnp.where(kappa > 0.0, 1.0, 0.0)

    for row in range(EXT):
        here = pl.ds(row * 8, 8)
        kappa = work_ref[here, :]
        mask = mask_of(kappa)
        if row + 1 < EXT:
            after = work_ref[pl.ds((row + 1) * 8, 8), :]
            along_ref[here, :] = 0.5 * (mask * after + kappa * mask_of(after))
        else:
            along_ref[here, :] = jnp.zeros((8, 128), F32)
        beside = pltpu.roll(kappa, 127, 1)
        across_ref[here, :] = 0.5 * (mask * beside + kappa * mask_of(beside))


def strips(packed):
    west, east = packed

    def west_of(level):
        return pltpu.roll(west, 128 - 32 * level, 1) if level else west

    def east_of(level):
        return pltpu.roll(east, (2 * 128 - HALO - 32 * level) % 128, 1)

    return west_of, east_of


def from_pairs(near_ref, far_ref, which):
    near, far = near_ref[which, pl.ds(0, EXT), :], far_ref[which, pl.ds(0, EXT), :]
    even = parity("ty")
    return jnp.where(even, far, near), jnp.where(even, near, far)


def send_segments(picked_ref, listed_ref, segments):
    listed = jnp.concatenate([listed_ref[...], jnp.zeros((128 - TX, 128), F32)], axis=0).T
    mine = listed[CAP : 2 * CAP].astype(jnp.int32)
    lane = iota((CAP, LEV * CX), 1)
    hits = [
        jnp.where(mine[:, source : source + 1] == lane, 1.0, 0.0) for source in range(TX)
    ]
    onehot = jnp.concatenate(hits, axis=0).astype(BF16)
    picked_ref[...] = pick(onehot, segments)


INNER = (SIDE - NSTEP, SIDE + CX + NSTEP)
OUTER = (SIDE - HALO, SIDE + CX + HALO)


def spread_first_kernel(
    count_ref, field_ref, kappa_ext_ref, near_ref, far_ref, sigma_ref, listed_ref, _,
    picked_ref, once_ref, twice_ref, along_ref, across_ref, work_ref,
):
    band = lax.axis_index("ty")
    west, east = from_pairs(near_ref, far_ref, 1)
    west = west * jnp.where(band > 0, 1.0, 0.0)
    east = east * jnp.where(band < TY - 1, 1.0, 0.0)
    widen(work_ref, kappa_ext_ref, *strips((west, east)))
    faces(work_ref, along_ref, across_ref)
    widen(work_ref, field_ref, *strips(from_pairs(near_ref, far_ref, 0)))
    counts = level_counts(count_ref)
    sweeps(work_ref, along_ref, across_ref, counts, *OUTER)
    for level in range(LEV):
        once_ref[level] = tile_part(work_ref, level)
    sweeps(work_ref, along_ref, across_ref, counts, *INNER)
    parts = []
    for level in range(LEV):
        part = tile_part(work_ref, level)
        twice_ref[level] = part
        parts.append(part * sigma_ref[level])
    send_segments(picked_ref, listed_ref, jnp.concatenate(parts, axis=0))


def spread_next_kernel(
    count_ref, field_ref, near_ref, far_ref, sigma_ref, listed_ref, along_ref, across_ref,
    once_ref, twice_ref,
    picked_ref, image_ref, work_ref,
):
    widen(work_ref, field_ref, *strips(from_pairs(near_ref, far_ref, 0)))
    counts = level_counts(count_ref)
    sweeps(work_ref, along_ref, across_ref, counts, *OUTER)
    for level in range(LEV):
        image_ref[level] = once_ref[level] + tile_part(work_ref, level)
    sweeps(work_ref, along_ref, across_ref, counts, *INNER)
    parts = []
    for level in range(LEV):
        parts.append((twice_ref[level] + tile_part(work_ref, level)) * sigma_ref[level])
    send_segments(picked_ref, listed_ref, jnp.concatenate(parts, axis=0))


def spread_last_kernel(count_ref, field_ref, near_ref, far_ref, along_ref, across_ref, last_ref, work_ref):
    widen(work_ref, field_ref, *strips(from_pairs(near_ref, far_ref, 0)))
    sweeps(work_ref, along_ref, across_ref, level_counts(count_ref), *INNER)
    for level in range(LEV):
        last_ref[level] = tile_part(work_ref, level)


def finish_kernel(
    last_ref, here_ref, one_ref, two_ref, three_ref, start_ref, image_ref, control_ref, residual_ref
):
    sums = (here_ref[...] + one_ref[...]) + (two_ref[...] + three_ref[...])
    sums = jnp.sum(sums, axis=1, keepdims=True)
    start_start = sums[0:1]
    start_image = sums[0:1] + sums[1:2]
    image_image = sums[2:3]
    image_second = sums[2:3] + sums[3:4]
    step = start_start / start_image
    norm = step * step * image_image - 2.0 * step * start_image + start_start
    ratio = norm / start_start
    next_next = start_image - 2.0 * step * image_image + step * step * image_second
    next_start = start_image - step * image_image
    curvature = next_next + 2.0 * ratio * next_start + ratio * ratio * start_image
    second = norm / curvature
    for level in range(LEV):
        start = start_ref[level]
        image = image_ref[level]
        twice = image + last_ref[level]
        remainder = start - step * image
        direction = remainder + ratio * start
        curved = (1.0 + ratio) * image - step * twice
        control_ref[level] = step * start + second * direction
        residual_ref[level] = remainder - second * curved


WORK = [pltpu.VMEM((EXT * 8 + 8, 128), F32)]
TILE = jax.ShapeDtypeStruct((LEV, CX, CY), F32)
WIDENED = jax.ShapeDtypeStruct((ROWS, 128), F32)
LAID = jax.ShapeDtypeStruct((EXT * 8, 128), F32)
TARGETS = jax.ShapeDtypeStruct((8, SLOTS), jnp.int32)
LISTS = jax.ShapeDtypeStruct((TX, 128), F32)
PICKED = jax.ShapeDtypeStruct((SLOTS, 128), F32)


def edge_shape(number, more=0):
    return jax.ShapeDtypeStruct((number, EXT + more, 128), F32)


def tile_call(kernel, out_shape, scalars, arrays, name, scratch=(), after=()):
    return pl.pallas_call(
        kernel,
        in_specs=[SCALARS] * len(scalars) + [HERE] * len(arrays) + [HERE] * len(after),
        out_specs=[HERE] * len(out_shape),
        out_shape=list(out_shape),
        scratch_shapes=list(scratch),
        compiler_params=pltpu.CompilerParams(vmem_limit_bytes=16 << 20),
        name=name,
    )(*scalars, *arrays, *after)


def swap_neighbours(for_pair, for_other, axis):
    count = lax.axis_size(axis)
    pairs = [(i, i ^ 1) for i in range(count)]
    others = [(i, (i + (1 if i % 2 else -1)) % count) for i in range(count)]
    return lax.ppermute(for_pair, axis, pairs), lax.ppermute(for_other, axis, others)


def exchange(parts):
    return lax.all_to_all(parts, "tx", split_axis=0, concat_axis=0, tiled=True)


def body(
    innovation,
    obs_weight,
    obs_operator,
    block_tile,
    owner_counts,
    block_column,
    sea_mask,
    diffusivity,
    background_std,
    step_counts,
):
    tile = block_tile.reshape(1, OWN)
    column = block_column.reshape(1, OWN)

    rows_shape = jax.ShapeDtypeStruct((2, LEV, SIDE, 128), F32)
    kappa, pair, other = tile_call(
        prepare_kernel,
        (TILE, rows_shape, rows_shape),
        (),
        (sea_mask, diffusivity, background_std),
        "prepare",
    )
    near_x, far_x = swap_neighbours(pair, other, "tx")
    parts, adjoint = run_first(owner_counts, tile, column, innovation, obs_weight, obs_operator)
    turned = run_turn(obs_operator)
    parts, turned = lax.optimization_barrier((exchange(parts), turned))
    field, sigma_ext, kappa_ext, pair, other, listed, rows = tile_call(
        open_kernel,
        (WIDENED, WIDENED, WIDENED, edge_shape(2), edge_shape(2), LISTS, TARGETS),
        (),
        (parts, background_std, kappa, near_x, far_x),
        "open_tile",
    )
    near, far = swap_neighbours(pair, other, "ty")
    brought = tile_call(bring_kernel, (SUMS,), (), (listed, turned), "bring_blocks")
    picked, once, twice, along, across = tile_call(
        spread_first_kernel,
        (PICKED, TILE, TILE, LAID, LAID),
        (step_counts,),
        (field, kappa_ext, near, far, background_std, listed),
        "spread_first",
        WORK,
        after=brought,
    )
    returned = exchange(picked.reshape(TX, CAP, 128)).reshape(SLOTS, 128)
    parts, adjoint, sums = run_middle(owner_counts, tile, obs_weight, returned, adjoint, turned)
    parts = exchange(parts)
    field, pair, other = tile_call(
        gather_kernel,
        (WIDENED, edge_shape(1), edge_shape(1)),
        (),
        (parts, sigma_ext, rows),
        "gather_tile",
    )
    near, far = swap_neighbours(pair, other, "ty")
    picked, image = tile_call(
        spread_next_kernel,
        (PICKED, TILE),
        (step_counts,),
        (field, near, far, background_std, listed, along, across, once, twice),
        "spread_next",
        WORK,
    )
    returned = exchange(picked.reshape(TX, CAP, 128)).reshape(SLOTS, 128)
    parts, adjoint, sums = run_middle(
        owner_counts, tile, obs_weight, returned, adjoint, turned, sums
    )
    parts = exchange(parts)
    field, pair, other, sums = tile_call(
        last_gather_kernel,
        (WIDENED, edge_shape(1, 8), edge_shape(1, 8), SUMS),
        (),
        (parts, sigma_ext, rows),
        "gather_last",
    )
    near, far = swap_neighbours(pair, other, "ty")
    chip = tile_call(meet_kernel, (SUMS,), (), (sums, near), "meet")[0]
    chips = [
        lax.ppermute(chip, "ty", [(i, i ^ k) for i in range(lax.axis_size("ty"))]) for k in (2, 4, 6)
    ]
    last = tile_call(
        spread_last_kernel,
        (TILE,),
        (step_counts,),
        (field, near, far, along, across),
        "spread_last",
        WORK,
    )[0]
    control_field, residual = tile_call(
        finish_kernel, (TILE, TILE), (), (last, chip, *chips, once, image), "finish"
    )
    return control_field, residual


def solution(mesh):
    placed = (
        P(("tx", "ty"), None),
        P(("tx", "ty"), None),
        P(("tx", "ty"), None, None),
        P(("tx", "ty"), None),
        P(("tx", "ty")),
        P(("tx", "ty")),
        P(None, "tx", "ty"),
        P(None, "tx", "ty"),
        P(None, "tx", "ty"),
        P(),
    )
    return jax.shard_map(
        body,
        mesh=mesh,
        in_specs=placed,
        out_specs=(P(None, "tx", "ty"), P(None, "tx", "ty")),
        check_vma=False,
    )
```
